32 devices in a mesh: dp: 2 (over core), mp: 16 (over z, y, x).
Axes of the slice: x: 2, y: 2, z: 4, core: 2. Of those that a mesh axis runs over, the one named last changes fastest.
Arguments:
- tokens: bfloat16 [8192, 1024], P(('dp', 'mp')), may hold values from -6 to 6
- cotangent: bfloat16 [8192, 1024], P(('dp', 'mp')), may hold values from -6 to 6
- seq_lengths: int32 [2, 4], P('dp'), may hold values from 1 to 2048, 4096 in all within a row
- first_gain: float32 [1024], replicated, may hold values from 0.1 to 1.9
- first_bias: float32 [1024], replicated, may hold values from -2 to 2
- second_gain: float32 [1024], replicated, may hold values from 0.1 to 1.9
- second_bias: float32 [1024], replicated, may hold values from -2 to 2
- blend_key: float32 [1024], replicated, may hold values from 0 to 1
- blend_value: float32 [1024], replicated, may hold values from 0 to 1
- blend_recept: float32 [1024], replicated, may hold values from 0 to 1
- channel_key: float32 [1024], replicated, may hold values from 0 to 1
- channel_recept: float32 [1024], replicated, may hold values from 0 to 1
- time_decay: float32 [1024], P('mp'), may hold values from -8 to -2
- time_first: float32 [1024], P('mp'), may hold values from -1 to 1
- weight_key: bfloat16 [1024, 1024], P(None, 'mp'), may hold values from -0.1875 to 0.1875
- weight_value: bfloat16 [1024, 1024], P(None, 'mp'), may hold values from -0.1875 to 0.1875
- weight_recept: bfloat16 [1024, 1024], P(None, 'mp'), may hold values from -0.1875 to 0.1875
- weight_output: bfloat16 [1024, 1024], P('mp'), may hold values from -0.75 to 0.75
- hidden_key: bfloat16 [1024, 4096], P(None, 'mp'), may hold values from -0.1875 to 0.1875
- hidden_value: bfloat16 [4096, 1024], P('mp'), may hold values from -0.09375 to 0.09375
- hidden_recept: bfloat16 [1024, 1024], P(None, 'mp'), may hold values from -0.1875 to 0.1875
Outputs:
- block_out: bfloat16 [8192, 1024], P(('dp', 'mp'))
- grad_tokens: float32 [8192, 1024], P(('dp', 'mp'))
- grad_first_gain: float32 [1024], replicated
- grad_first_bias: float32 [1024], replicated
- grad_second_gain: float32 [1024], replicated
- grad_second_bias: float32 [1024], replicated
- grad_blend_key: float32 [1024], replicated
- grad_blend_value: float32 [1024], replicated
- grad_blend_recept: float32 [1024], replicated
- grad_channel_key: float32 [1024], replicated
- grad_channel_recept: float32 [1024], replicated
- grad_time_decay: float32 [1024], P('mp')
- grad_time_first: float32 [1024], P('mp')
- grad_weight_key: float32 [1024, 1024], P(None, 'mp')
- grad_weight_value: float32 [1024, 1024], P(None, 'mp')
- grad_weight_recept: float32 [1024, 1024], P(None, 'mp')
- grad_weight_output: float32 [1024, 1024], P('mp')
- grad_hidden_key: float32 [1024, 4096], P(None, 'mp')
- grad_hidden_value: float32 [4096, 1024], P('mp')
- grad_hidden_recept: float32 [1024, 1024], P(None, 'mp')
The draws below stay inside these ranges and needn't reach their ends.
Inputs may be any that keep to these rules, and one draw needn't show every extreme that they name: `seq_lengths`: each row sums to 4096; its largest entry is exactly 2048.
All inputs are finite; a program needn't handle non-finite values.
Results may differ from the reference program's by a relative error of at most 0.03.
Values may be sent and summed in bfloat16 or wider, within the bound.
No kernel may reach another device: no remote copies, remote signals or barrier semaphores. Data moves between devices by JAX's collectives and lax.ppermute only.
A program may use at most 576 MiB of HBM per device.

```python
import math
import jax
import jax.numpy as jnp
import numpy as np
from jax import lax

D = 1024
DFF = 4096
NSEQ = 4
GROUP = 4096
GROUPS = 2
TOKENS = 8192


def level_of(key, extent, pieces, smallest, largest):
    factor_of = 1.0
    for dim, blocks in pieces:
        steps = jax.random.uniform(jax.random.fold_in(jax.random.fold_in(key, 6), dim), (blocks,), jnp.float32, smallest / len(pieces), largest / len(pieces))
        factor_of = factor_of * jnp.repeat(jnp.exp(steps), extent[dim] // blocks).reshape((-1,) + (1,) * (len(extent) - 1 - dim))
    return factor_of


def length_profile(count, total, reach, skew):
    weights = [(1 << 20) // math.isqrt(standing ** skew) + 1 for standing in range(2, count + 1)]
    spare, holding = total - reach - (count - 1), [1] * (count - 1)
    while spare > 0:
        free = [i for i in range(count - 1) if holding[i] < reach]
        whole, budget = sum([weights[i] for i in free]), spare
        for i in free:
            more = min(reach - holding[i], max(1, budget * weights[i] // whole), spare)
            holding[i] = holding[i] + more
            spare = spare - more
    return np.array([reach] + holding)


def ragged_sizes(key, amount, total, bound, lean):
    if amount == 2:
        one = jax.random.randint(key, (), max(1, total - bound), min(bound, total - 1) + 1)
        return jnp.stack([one, total - one])
    sizes = jnp.asarray(length_profile(amount, total, bound, lean), jnp.int32)
    couples = (amount - 1) // 2
    giver, sink = sizes[1:1 + 2 * couples:2], sizes[2:2 + 2 * couples:2]
    room = jnp.minimum(giver - 1, bound - sink)
    moved = jax.random.randint(jax.random.fold_in(key, 1), (couples,), 0, 1 << 20) % (room + 1)
    sizes = sizes.at[1:1 + 2 * couples:2].set(giver - moved).at[2:2 + 2 * couples:2].set(sink + moved)
    return sizes[jax.random.permutation(jax.random.fold_in(key, 2), amount)]


def normal_values(own_key, dims, scale, limit, split=(), kind=jnp.bfloat16):
    gain = level_of(own_key, dims, split, -0.22, 0.18) if split else 1.0
    values = jax.random.normal(own_key, dims, jnp.float32) * scale * gain
    return jnp.minimum(jnp.maximum(values, -limit), limit).astype(kind)


def setup_inputs(seed: int = 0) -> dict:
    seeds = jax.random.split(jax.random.key(seed), 22)
    tokens = normal_values(seeds[0], (TOKENS, D), 1.0, 6.0, ((0, 32),))
    cotangent = normal_values(seeds[1], (TOKENS, D), 1.0, 6.0, ((0, 32),))
    seq_lengths = jax.vmap(lambda own: ragged_sizes(own, NSEQ, GROUP, GROUP // 2, 2))(jax.random.split(seeds[2], GROUPS)).reshape((GROUPS, NSEQ)).astype(jnp.int32)
    first_gain = jnp.clip(1.0 + 0.18 * jax.random.normal(seeds[3], (D,), jnp.float32), 0.1, 1.9)
    first_bias = normal_values(seeds[4], (D,), 0.4, 2.0, (), jnp.float32)
    second_gain = jnp.clip(1.0 + 0.18 * jax.random.normal(seeds[5], (D,), jnp.float32), 0.1, 1.9)
    second_bias = normal_values(seeds[6], (D,), 0.4, 2.0, (), jnp.float32)
    blend_key = jnp.clip(jax.random.uniform(seeds[7], (D,), jnp.float32, 0.0, 1.0), 0.0, 1.0)
    blend_value = jnp.clip(jax.random.uniform(seeds[8], (D,), jnp.float32, 0.0, 1.0), 0.0, 1.0)
    blend_recept = jnp.clip(jax.random.uniform(seeds[9], (D,), jnp.float32, 0.0, 1.0), 0.0, 1.0)
    channel_key = jnp.clip(jax.random.uniform(seeds[10], (D,), jnp.float32, 0.0, 1.0), 0.0, 1.0)
    channel_recept = jnp.clip(jax.random.uniform(seeds[11], (D,), jnp.float32, 0.0, 1.0), 0.0, 1.0)
    time_decay = jnp.clip(-8.0 + 6.0 * jax.random.uniform(seeds[12], (D,), jnp.float32) ** level_of(seeds[12], (D,), ((0, 16),), -0.2, 0.2), -8.0, -2.0)
    time_first = jnp.clip(jax.random.uniform(seeds[13], (D,), jnp.float32, -1.0, 1.0) * level_of(seeds[13], (D,), ((0, 16),), -0.4, 0.0), -1.0, 1.0)
    weight_key = normal_values(seeds[14], (D, D), D ** -0.5, 0.1875, ((1, 16),))
    weight_value = normal_values(seeds[15], (D, D), D ** -0.5, 0.1875, ((1, 16),))
    weight_recept = normal_values(seeds[16], (D, D), D ** -0.5, 0.1875, ((1, 16),))
    weight_output = normal_values(seeds[17], (D, D), (D // 16) ** -0.5, 0.75, ((0, 16),))
    hidden_key = normal_values(seeds[18], (D, DFF), D ** -0.5, 0.1875, ((1, 16),))
    hidden_value = normal_values(seeds[19], (DFF, D), DFF ** -0.5, 0.09375, ((0, 16),))
    hidden_recept = normal_values(seeds[20], (D, D), D ** -0.5, 0.1875, ((1, 16),))
    return dict(tokens=tokens, cotangent=cotangent, seq_lengths=seq_lengths, first_gain=first_gain, first_bias=first_bias, second_gain=second_gain, second_bias=second_bias, blend_key=blend_key, blend_value=blend_value, blend_recept=blend_recept, channel_key=channel_key, channel_recept=channel_recept, time_decay=time_decay, time_first=time_first, weight_key=weight_key, weight_value=weight_value, weight_recept=weight_recept, weight_output=weight_output, hidden_key=hidden_key, hidden_value=hidden_value, hidden_recept=hidden_recept)


@jax.custom_vjp
def low(v):
    return lax.optimization_barrier(v.astype(jnp.bfloat16)).astype(jnp.float32)

@jax.custom_vjp
def low_back(v):
    return v

def low_keep(v):
    return (low(v), None)

def low_pass(kept, grad):
    return (grad,)

def back_keep(v):
    return (v, None)

def back_low(kept, grad):
    return (low(grad),)
low.defvjp(low_keep, low_pass)
low_back.defvjp(back_keep, back_low)
norm_eps = 1e-05

def matmul(left, right):
    return jnp.dot(left, right, precision=lax.Precision.HIGHEST)

def layer_norm(source, norm_gain, norm_bias):
    centre = lax.optimization_barrier(jnp.mean(source, axis=-1, keepdims=True))
    spread = source - centre
    scaled = spread * lax.rsqrt(lax.optimization_barrier(jnp.mean(spread * spread, axis=-1, keepdims=True)) + norm_eps)
    return scaled * norm_gain + norm_bias

def previous(source, keep_flag):
    moved = jnp.concatenate([jnp.zeros_like(source[:1]), source[:-1]], axis=0)
    return moved * keep_flag

def blend(present_memory, before, factor):
    return present_memory * factor + before * (1.0 - factor)

def scaled_payload_prefix(lookup_lines, payload_table, fading_speed, reward_coefficient, series_opening_markers):
    factor = jnp.exp(-jnp.exp(fading_speed))

    def advance(carry, entry):
        numer, denom = carry
        lookup_line_window, value_row, flag_row = entry
        numer = jnp.where(flag_row, jnp.zeros_like(numer), numer)
        denom = jnp.where(flag_row, jnp.zeros_like(denom), denom)
        present_memory = jnp.exp(reward_coefficient + lookup_line_window)
        result = (numer + present_memory * value_row) / (denom + present_memory)
        growth = jnp.exp(lookup_line_window)
        return ((factor * numer + growth * value_row, factor * denom + growth), result)
    start_state = (jnp.zeros_like(lookup_lines[0]), jnp.zeros_like(lookup_lines[0]))
    _, mixed = lax.scan(advance, start_state, (lookup_lines, payload_table, series_opening_markers))
    return mixed

def block(source, params, keep_flag, series_opening_markers):
    first_gain, first_bias, second_gain, second_bias, blend_key, blend_value, blend_recept, channel_key, channel_recept, time_decay, time_first, weight_key, weight_value, weight_recept, weight_output, hidden_key, hidden_value, hidden_recept = params
    normed = low(layer_norm(source, first_gain, first_bias))
    before = previous(normed, keep_flag)
    mix_key_in = low(blend(normed, before, blend_key))
    mix_value_in = low(blend(normed, before, blend_value))
    mix_recept_in = low(blend(normed, before, blend_recept))
    lookup_lines = low_back(matmul(mix_key_in, weight_key))
    payload_table = low_back(matmul(mix_value_in, weight_value))
    recept = low_back(matmul(mix_recept_in, weight_recept))
    mixed = scaled_payload_prefix(lookup_lines, payload_table, time_decay, time_first, series_opening_markers)
    gated = low(jax.nn.sigmoid(recept) * mixed)
    hidden_state = source + low_back(matmul(gated, weight_output))
    normed_two = low(layer_norm(hidden_state, second_gain, second_bias))
    before_two = previous(normed_two, keep_flag)
    ffn_key_in = low(blend(normed_two, before_two, channel_key))
    ffn_recept_in = low(blend(normed_two, before_two, channel_recept))
    ffn_pre = low_back(matmul(ffn_key_in, hidden_key))
    squared = low(jnp.square(jax.nn.relu(ffn_pre)))
    carried = low_back(matmul(squared, hidden_value))
    ffn_gate = jax.nn.sigmoid(low_back(matmul(ffn_recept_in, hidden_recept)))
    return hidden_state + ffn_gate * carried

def sequence_masks(lengths):
    places = jnp.arange(GROUP, dtype=jnp.int32)
    ends = jnp.cumsum(lengths).astype(jnp.int32)
    opening_markers = lax.optimization_barrier(jnp.sum(jnp.where(ends[None, :] <= places[:, None], lengths[None, :], 0), axis=1)).astype(jnp.int32)
    return (places == opening_markers, (places > opening_markers).astype(jnp.float32)[:, None])

def reference(tokens, cotangent, seq_lengths, first_gain, first_bias, second_gain, second_bias, blend_key, blend_value, blend_recept, channel_key, channel_recept, time_decay, time_first, weight_key, weight_value, weight_recept, weight_output, hidden_key, hidden_value, hidden_recept):
    params = tuple((entry.astype(jnp.float32) for entry in (first_gain, first_bias, second_gain, second_bias, blend_key, blend_value, blend_recept, channel_key, channel_recept, time_decay, time_first, weight_key, weight_value, weight_recept, weight_output, hidden_key, hidden_value, hidden_recept)))
    stream = tokens.astype(jnp.float32).reshape(GROUPS, GROUP, D)
    grad_stream = cotangent.astype(jnp.float32).reshape(GROUPS, GROUP, D)

    def one_group(running, entry):
        source, grad_source, lengths = entry
        series_opening_markers, keep_flag = sequence_masks(lengths)

        def forward(rows_in, *weights):
            return block(rows_in, weights, keep_flag, series_opening_markers)
        result, backward = jax.vjp(forward, source, *params)
        grads = backward(grad_source)
        running = tuple((left + right for left, right in zip(running, grads[1:])))
        return (running, (result.astype(jnp.bfloat16), grads[0]))
    initial = tuple((jnp.zeros_like(entry) for entry in params))
    totals, (outputs, grad_rows) = lax.scan(one_group, initial, (stream, grad_stream, seq_lengths))
    return (outputs.reshape(TOKENS, D), grad_rows.reshape(TOKENS, D)) + totals
```

```python
import functools

import jax
import jax.numpy as jnp
from jax import lax
from jax.experimental import pallas as pl
from jax.experimental.pallas import tpu as pltpu
from jax.sharding import PartitionSpec as P

norm_eps = 1e-05
f32 = jnp.float32
bf16 = jnp.bfloat16


def bits_of(count):
    total = count.bit_length() - 1
    cube = (0, 2, 4) if total == 5 else (0, 1, 2)
    pre = tuple(b for b in range(total) if b not in cube)
    return pre, cube


def swap(value, bit):
    count = lax.axis_size("mp")
    return lax.ppermute(value, "mp", [(i, i ^ (1 << bit)) for i in range(count)])


def swap_core(value):
    count = lax.axis_size("dp")
    return lax.ppermute(value, "dp", [(i, i ^ 1) for i in range(count)])


def relative_ids(count):
    pre, (a, b, c) = bits_of(count)
    low = [0]
    for bit in pre:
        low = low + [i ^ (1 << bit) for i in low]
    x, y, z = 1 << a, 1 << b, 1 << c
    return [k ^ i for k in (0, x, y, z, x ^ y, y ^ z, x ^ z, x ^ y ^ z) for i in low]


def gather_chunk(part):
    pre, (a, b, c) = bits_of(lax.axis_size("mp"))
    v = part[None]
    for bit in pre:
        v = jnp.concatenate([v, swap(v, bit)], 0)
    vx, vy, vz = swap(v, a), swap(v, b), swap(v, c)
    xy, yz, xz = swap(vy, a), swap(vz, b), swap(vx, c)
    half = v.shape[0] // 2
    one, two = swap(yz[:half], a), swap(xz[half:], b)
    return jnp.concatenate([v, vx, vy, vz, xy, yz, xz, one, two], 0)


def scatter_chunk(part):
    count = lax.axis_size("mp")
    pre, (a, b, c) = bits_of(count)
    p = part.reshape((8, count // 8) + part.shape[1:])
    half = p.shape[1] // 2
    one, two = swap(p[7, :half], a), swap(p[7, half:], b)
    yz = jnp.concatenate([p[5, :half] + one, p[5, half:]], 0)
    xz = jnp.concatenate([p[6, :half], p[6, half:] + two], 0)
    y = p[2] + swap(p[4], a)
    z = p[3] + swap(yz, b)
    x = p[1] + swap(xz, c)
    v = p[0] + swap(x, a) + swap(y, b) + swap(z, c)
    for bit in reversed(pre):
        half = v.shape[0] // 2
        v = v[:half] + swap(v[half:], bit)
    return v[0]


def gather_small(value):
    count = lax.axis_size("mp")
    v = value[None]
    for bit in range(count.bit_length() - 1):
        v = jnp.concatenate([v, swap(v, bit)], 0)
    return v


def total_small(value):
    for axis in ("mp", "dp"):
        count = lax.axis_size(axis)
        for bit in range(count.bit_length() - 1):
            value = value + lax.ppermute(value, axis, [(i, i ^ (1 << bit)) for i in range(count)])
    return value


ANY = pl.BlockSpec(memory_space=pl.ANY)
SMEM = pl.BlockSpec(memory_space=pltpu.SMEM)


def place_kernel(pieces, count, places_ref, own_ref, other_ref, *rest):
    outs, sem = rest[:-1], rest[-1]
    copies = []
    for (offset, rows), out in zip(pieces, outs):
        for side, source in enumerate((own_ref, other_ref)):
            for j in range(count):
                target = pl.multiple_of(places_ref[side, j] * rows, 16)
                copies.append(
                    pltpu.make_async_copy(
                        source.at[j, pl.ds(offset, rows), :],
                        out.at[pl.ds(target, rows), :],
                        sem.at[len(copies)],
                    )
                )
    for copy in copies:
        copy.start()
    for copy in copies:
        copy.wait()


def place(own, other, places, pieces):
    count, _, width = own.shape
    return pl.pallas_call(
        functools.partial(place_kernel, pieces, count),
        out_shape=tuple(
            jax.ShapeDtypeStruct((2 * count * rows, width), own.dtype) for _, rows in pieces
        ),
        in_specs=[SMEM, ANY, ANY],
        out_specs=tuple(ANY for _ in pieces),
        scratch_shapes=[pltpu.SemaphoreType.DMA((2 * count * len(pieces),))],
    )(places, own, other)


def unplace_kernel(pieces, count, places_ref, *rest):
    sources, (own_ref, other_ref, sem) = rest[:-3], rest[-3:]
    copies = []
    for (offset, rows), source in zip(pieces, sources):
        for side, out in enumerate((own_ref, other_ref)):
            for j in range(count):
                start = pl.multiple_of(places_ref[side, j] * rows, 16)
                copies.append(
                    pltpu.make_async_copy(
                        source.at[pl.ds(start, rows), :],
                        out.at[j, pl.ds(offset, rows), :],
                        sem.at[len(copies)],
                    )
                )
    for copy in copies:
        copy.start()
    for copy in copies:
        copy.wait()


def unplace(matrices, places, pieces, count):
    width = matrices[0].shape[1]
    height = sum(rows for _, rows in pieces)
    shape = jax.ShapeDtypeStruct((count, height, width), matrices[0].dtype)
    return pl.pallas_call(
        functools.partial(unplace_kernel, pieces, count),
        out_shape=(shape, shape),
        in_specs=[SMEM] + [ANY] * len(matrices),
        out_specs=(ANY, ANY),
        scratch_shapes=[pltpu.SemaphoreType.DMA((2 * count * len(pieces),))],
    )(places, *matrices)


def tile_down(value_a, value_b, cols, powers):
    for k in range(3):
        factor = powers[k] * cols[:, k : k + 1]
        value_a = value_a + factor * pltpu.roll(value_a, 1 << k, 0)
        value_b = value_b + factor * pltpu.roll(value_b, 1 << k, 0)
    return value_a, value_b


def tile_up(value_a, value_b, cols, powers):
    for k in range(3):
        factor = powers[k] * cols[:, k : k + 1]
        value_a = value_a + factor * pltpu.roll(value_a, 8 - (1 << k), 0)
        value_b = value_b + factor * pltpu.roll(value_b, 8 - (1 << k), 0)
    return value_a, value_b


def forward_end_kernel(k_ref, v_ref, cols_ref, decay_ref, out_ref):
    rows, width = k_ref.shape
    rate = jnp.exp(decay_ref[0:1, :])
    powers = [jnp.exp(-rate * (1 << k)) for k in range(3)]
    climb = lax.broadcasted_iota(jnp.int32, (8, width), 0).astype(f32) + 1.0
    full = jnp.exp(-rate * climb)

    def body(t, carry):
        at = pl.ds(pl.multiple_of(t * 8, 8), 8)
        cols = cols_ref[at, :]
        growth = jnp.exp(k_ref[at, :])
        ya, yb = tile_down(growth * v_ref[at, :], growth, cols, powers)
        reach = full * cols[:, 3:4]
        ya = ya + reach * carry[0]
        yb = yb + reach * carry[1]
        return ya[7:8, :], yb[7:8, :]

    zero = jnp.zeros((1, width), f32)
    ya, yb = lax.fori_loop(0, rows // 8, body, (zero, zero))
    out_ref[0:1, :] = ya
    out_ref[1:2, :] = yb


def forward_kernel(k_ref, v_ref, r_ref, cols_ref, decay_ref, enter_ref, gated_ref, mixed_ref, a_ref, b_ref):
    rows, width = k_ref.shape
    rate = jnp.exp(decay_ref[0:1, :])
    bonus = decay_ref[1:2, :]
    powers = [jnp.exp(-rate * (1 << k)) for k in range(3)]
    place_in = lax.broadcasted_iota(jnp.int32, (8, width), 0)
    full = jnp.exp(-rate * (place_in.astype(f32) + 1.0))

    def body(t, carry):
        at = pl.ds(pl.multiple_of(t * 8, 8), 8)
        cols = cols_ref[at, :]
        keys = k_ref[at, :]
        values = v_ref[at, :]
        growth = jnp.exp(keys)
        ya, yb = tile_down(growth * values, growth, cols, powers)
        reach = full * cols[:, 3:4]
        ya = ya + reach * carry[0]
        yb = yb + reach * carry[1]
        keep = cols[:, 4:5]
        sa = keep * jnp.where(place_in == 0, carry[0], pltpu.roll(ya, 1, 0))
        sb = keep * jnp.where(place_in == 0, carry[1], pltpu.roll(yb, 1, 0))
        now = jnp.exp(bonus + keys)
        mixed = (sa + now * values) / (sb + now)
        a_ref[at, :] = sa
        b_ref[at, :] = sb
        mixed_ref[at, :] = mixed
        gated_ref[at, :] = jax.nn.sigmoid(r_ref[at, :]) * mixed
        return ya[7:8, :], yb[7:8, :]

    lax.fori_loop(0, rows // 8, body, (enter_ref[0:1, :], enter_ref[1:2, :]))


def backward_end_kernel(g_ref, k_ref, mixed_ref, b_ref, cols_ref, decay_ref, out_ref):
    rows, width = k_ref.shape
    rate = jnp.exp(decay_ref[0:1, :])
    bonus = decay_ref[1:2, :]
    powers = [jnp.exp(-rate * (1 << k)) for k in range(3)]
    place_in = lax.broadcasted_iota(jnp.int32, (8, width), 0)
    full = jnp.exp(-rate * (8.0 - place_in.astype(f32)))
    tiles = rows // 8

    def body(step, carry):
        at = pl.ds(pl.multiple_of((tiles - 1 - step) * 8, 8), 8)
        cols = cols_ref[at, :]
        now = jnp.exp(bonus + k_ref[at, :])
        xa = g_ref[at, :] / (b_ref[at, :] + now)
        ya, yb = tile_up(xa, -xa * mixed_ref[at, :], cols, powers)
        reach = full * cols[:, 3:4]
        ya = ya + reach * carry[0]
        yb = yb + reach * carry[1]
        return ya[0:1, :], yb[0:1, :]

    zero = jnp.zeros((1, width), f32)
    ya, yb = lax.fori_loop(0, tiles, body, (zero, zero))
    out_ref[0:1, :] = ya
    out_ref[1:2, :] = yb


def backward_kernel(
    g_ref, k_ref, v_ref, mixed_ref, a_ref, b_ref, cols_ref, decay_ref, enter_ref, gk_ref, gv_ref, small_ref
):
    rows, width = k_ref.shape
    rate = jnp.exp(decay_ref[0:1, :])
    bonus = decay_ref[1:2, :]
    powers = [jnp.exp(-rate * (1 << k)) for k in range(3)]
    place_in = lax.broadcasted_iota(jnp.int32, (8, width), 0)
    full = jnp.exp(-rate * (8.0 - place_in.astype(f32)))
    tiles = rows // 8

    def body(step, carry):
        at = pl.ds(pl.multiple_of((tiles - 1 - step) * 8, 8), 8)
        cols = cols_ref[at, :]
        keys = k_ref[at, :]
        values = v_ref[at, :]
        mixed = mixed_ref[at, :]
        sa, sb = a_ref[at, :], b_ref[at, :]
        now = jnp.exp(bonus + keys)
        growth = jnp.exp(keys)
        xa = g_ref[at, :] / (sb + now)
        ya, yb = tile_up(xa, -xa * mixed, cols, powers)
        reach = full * cols[:, 3:4]
        ya = ya + reach * carry[0]
        yb = yb + reach * carry[1]
        keep = cols[:, 4:5]
        after_a = keep * jnp.where(place_in == 7, carry[0], pltpu.roll(ya, 7, 0))
        after_b = keep * jnp.where(place_in == 7, carry[1], pltpu.roll(yb, 7, 0))
        share = xa * now
        bend = share * (values - mixed)
        gv_ref[at, :] = share + after_a * growth
        gk_ref[at, :] = bend + growth * (after_a * values + after_b)
        return (
            ya[0:1, :],
            yb[0:1, :],
            carry[2] + bend,
            carry[3] + after_a * sa + after_b * sb,
        )

    zero = jnp.zeros((8, width), f32)
    done = lax.fori_loop(0, tiles, body, (enter_ref[0:1, :], enter_ref[1:2, :], zero, zero))
    small_ref[0:1, :] = jnp.sum(done[3], axis=0, keepdims=True) * (-rate * jnp.exp(-rate))
    small_ref[1:2, :] = jnp.sum(done[2], axis=0, keepdims=True)


def call_whole(kernel, outs, *args):
    return pl.pallas_call(
        kernel,
        out_shape=outs,
        in_specs=[pl.BlockSpec(memory_space=pltpu.VMEM)] * len(args),
        out_specs=jax.tree.map(lambda _: pl.BlockSpec(memory_space=pltpu.VMEM), outs),
        compiler_params=pltpu.CompilerParams(vmem_limit_bytes=40 * 2**20),
    )(*args)


def dot(left, right):
    return jnp.dot(left, right, preferred_element_type=f32)


def outer_sum(left, right):
    return lax.dot_general(left, right, (((0,), (0,)), ((), ())), preferred_element_type=f32)


def against(left, weight):
    return lax.dot_general(left, weight, (((1,), (1,)), ((), ())), preferred_element_type=f32)


def normalize(source):
    centre = jnp.mean(source, axis=-1, keepdims=True)
    spread = source - centre
    inverse = lax.rsqrt(jnp.mean(spread * spread, axis=-1, keepdims=True) + norm_eps)
    return spread * inverse, inverse


def blend_pair(present, before, factor):
    return (present.astype(f32) * factor + before * (1.0 - factor)).astype(bf16)


def norm_back(grad, scaled, inverse, gain):
    h = grad * gain
    return inverse * (
        h
        - jnp.mean(h, axis=-1, keepdims=True)
        - scaled * jnp.mean(h * scaled, axis=-1, keepdims=True)
    )


def shards(
    tokens,
    cotangent,
    seq_lengths,
    first_gain,
    first_bias,
    second_gain,
    second_bias,
    blend_key,
    blend_value,
    blend_recept,
    channel_key,
    channel_recept,
    time_decay,
    time_first,
    weight_key,
    weight_value,
    weight_recept,
    weight_output,
    hidden_key,
    hidden_value,
    hidden_recept,
):
    count = lax.axis_size("mp")
    me = lax.axis_index("mp")
    core = lax.rem(lax.axis_index("dp"), 2)
    rows, width = tokens.shape
    group_rows = rows * count
    chan = weight_key.shape[1]
    units = hidden_key.shape[1]
    hc, hu = chan // 2, units // 2
    ids = relative_ids(count)
    shift_down = [(i, i + 1) for i in range(count - 1)]
    shift_up = [(i + 1, i) for i in range(count - 1)]

    def half_rows(matrix, size):
        return lax.dynamic_slice_in_dim(matrix, core * size, size, 0)

    def half_cols(matrix, size):
        return lax.dynamic_slice_in_dim(matrix, core * size, size, 1).T

    chunk_a = jnp.concatenate(
        [
            half_cols(weight_key, hc),
            half_cols(weight_value, hc),
            half_cols(weight_recept, hc),
            half_rows(weight_output, hc),
        ],
        0,
    )
    chunk_b = jnp.concatenate([half_cols(hidden_key, hu), half_cols(hidden_recept, hc)], 0)
    chunk_c = half_rows(hidden_value, hu)
    own_a = gather_chunk(chunk_a)
    own_b = gather_chunk(chunk_b)
    own_c = gather_chunk(chunk_c)
    other_a, other_b, other_c = swap_core(own_a), swap_core(own_b), swap_core(own_c)
    ids_array = jnp.array(ids, jnp.int32)
    owners = jnp.bitwise_xor(ids_array, me)
    places = jnp.stack([owners * 2 + core, owners * 2 + 1 - core]).astype(jnp.int32)

    lengths = seq_lengths[0]
    ends = jnp.cumsum(lengths)

    def start_of(place):
        return jnp.sum(jnp.where(ends <= place[..., None], lengths, 0), axis=-1)

    def keep_of(place):
        return ((place > start_of(place)) & (place < group_rows)).astype(f32)

    here = me * rows + jnp.arange(rows, dtype=jnp.int32)
    keep_flat = keep_of(here)
    keep = keep_flat[:, None]
    keep_next = keep_of(here + 1)
    tiles = rows // 8

    def tile_cols(flags, up):
        f = flags.reshape(tiles, 8)
        if up:
            f = f[:, ::-1]
        one = f * (jnp.arange(8) >= 1)
        two = f * jnp.roll(f, 1, 1) * (jnp.arange(8) >= 2)
        four = f * jnp.roll(f, 1, 1) * jnp.roll(f, 2, 1) * jnp.roll(f, 3, 1) * (jnp.arange(8) >= 4)
        through = jnp.cumprod(f, axis=1)
        cols = jnp.stack([one, two, four, through, f, f, f, f], axis=-1)
        if up:
            cols = cols[:, ::-1]
        return cols.reshape(rows, 8)

    cols_down = tile_cols(keep_flat, False)
    cols_up = tile_cols(keep_next, True)

    small_rates = gather_small(jnp.stack([time_decay, time_first]))
    order = jnp.bitwise_xor(jnp.arange(count, dtype=jnp.int32), me)
    rates = jnp.moveaxis(jnp.take(small_rates, order, axis=0), 0, 1).reshape(2, width)
    rate = jnp.exp(rates[0])

    source = tokens.astype(f32)
    edge_row = lax.ppermute(tokens[-1:], "mp", shift_down).astype(f32)
    scaled_one, inverse_one = normalize(source)
    normed = (scaled_one * first_gain + first_bias).astype(bf16)
    edge = (normalize(edge_row)[0] * first_gain + first_bias).astype(bf16)
    before = jnp.concatenate([edge, normed[:-1]], 0).astype(f32) * keep
    mix_key = blend_pair(normed, before, blend_key)
    mix_value = blend_pair(normed, before, blend_value)
    mix_recept = blend_pair(normed, before, blend_recept)

    key_t, value_t, recept_t, output_w = place(
        own_a, other_a, places, ((0, hc), (hc, hc), (2 * hc, hc), (3 * hc, hc))
    )
    keys = against(mix_key, key_t)
    values = against(mix_value, value_t)
    recept = against(mix_recept, recept_t)

    pair = jax.ShapeDtypeStruct((2, width), f32)
    field = jax.ShapeDtypeStruct((rows, width), f32)
    sources = jnp.bitwise_xor(jnp.arange(count, dtype=jnp.int32), me)

    def fold(ends_all, valid, distance):
        weight = jnp.where(
            valid[:, None], jnp.exp(-rate[None] * (rows * distance[:, None]).astype(f32)), 0.0
        )
        return jnp.sum(ends_all * weight[:, None], axis=0)

    out_end = call_whole(forward_end_kernel, pair, keys, values, cols_down, rates)
    enter = fold(
        gather_small(out_end),
        (sources < me) & (start_of(me * rows - 1) < rows * (sources + 1)),
        jnp.maximum(me - 1 - sources, 0),
    )
    gated_full, mixed, state_a, state_b = call_whole(
        forward_kernel, (field, field, field, field), keys, values, recept, cols_down, rates, enter
    )
    gated = gated_full.astype(bf16)
    opened = jax.nn.sigmoid(recept)

    hidden = source + dot(gated, output_w)
    scaled_two, inverse_two = normalize(hidden)
    low = (scaled_two * second_gain + second_bias).astype(bf16)
    edge_two = lax.ppermute(low[-1:], "mp", shift_down)
    prior = jnp.concatenate([edge_two, low[:-1]], 0).astype(f32) * keep
    ffn_key_in = blend_pair(low, prior, channel_key)
    ffn_recept_in = blend_pair(low, prior, channel_recept)
    (hidden_recept_t,) = place(own_b, other_b, places, ((hu, hc),))
    hidden_key_t = jnp.concatenate([own_b[:, :hu], other_b[:, :hu]], 0).reshape(-1, width)
    hidden_value_w = jnp.concatenate([own_c, other_c], 0).reshape(-1, width)
    ffn_relu = jax.nn.relu(against(ffn_key_in, hidden_key_t))
    squared = jnp.square(ffn_relu).astype(bf16)
    gate = jax.nn.sigmoid(against(ffn_recept_in, hidden_recept_t))
    grad_out = cotangent.astype(f32)
    grad_carried = (grad_out * gate).astype(bf16)

    def split(matrix, size):
        parts = matrix.astype(bf16).reshape(2, count, size, width)
        return parts[0], parts[1]

    def reduce_chunk(own, other):
        return scatter_chunk(own + swap_core(other))

    g_value_own, g_value_other = split(outer_sum(squared, grad_carried), hu)
    sum_c = reduce_chunk(g_value_own, g_value_other)

    carried = dot(squared, hidden_value_w)
    block_out = (hidden + gate * carried).astype(bf16)
    grad_gate_pre = (grad_out * carried * gate * (1.0 - gate)).astype(bf16)
    grad_pre = (against(grad_carried, hidden_value_w) * 2.0 * ffn_relu).astype(bf16)
    g_key_own, g_key_other = split(outer_sum(grad_pre, ffn_key_in), hu)
    g_recept_own, g_recept_other = unplace(
        [outer_sum(grad_gate_pre, ffn_recept_in).astype(bf16)], places, ((0, hc),), count
    )
    sum_b = reduce_chunk(
        jnp.concatenate([g_key_own, g_recept_own], 1), jnp.concatenate([g_key_other, g_recept_other], 1)
    )
    grad_key_two = dot(grad_pre, hidden_key_t)
    grad_recept_two = dot(grad_gate_pre, hidden_recept_t)

    def blend_back(present, earlier, grads, factors):
        direct = sum(g * f for g, f in zip(grads, factors))
        spill = sum(g * (1.0 - f) for g, f in zip(grads, factors)) * keep
        tail = lax.ppermute(spill[:1], "mp", shift_up)
        change = present.astype(f32) - earlier
        totals = [jnp.sum(g * change, axis=0) for g in grads]
        return direct + jnp.concatenate([spill[1:], tail], 0), totals

    grad_second, ffn_small = blend_back(
        low, prior, (grad_key_two, grad_recept_two), (channel_key, channel_recept)
    )
    grad_second_gain = jnp.sum(grad_second * scaled_two, axis=0)
    grad_second_bias = jnp.sum(grad_second, axis=0)
    grad_hidden = grad_out + norm_back(grad_second, scaled_two, inverse_two, second_gain)
    grad_attended = grad_hidden.astype(bf16)

    g_output = outer_sum(gated, grad_attended).astype(bf16)
    grad_gated = against(grad_attended, output_w)
    grad_mixed = grad_gated * opened
    grad_recept = (grad_gated * mixed * opened * (1.0 - opened)).astype(bf16)
    back_end = call_whole(
        backward_end_kernel, pair, grad_mixed, keys, mixed, state_b, cols_up, rates
    )
    enter_back = fold(
        gather_small(back_end),
        (sources > me) & (start_of(sources * rows) <= rows * (me + 1)),
        jnp.maximum(sources - 1 - me, 0),
    )
    grad_keys_full, grad_values_full, rate_small = call_whole(
        backward_kernel,
        (field, field, pair),
        grad_mixed,
        keys,
        values,
        mixed,
        state_a,
        state_b,
        cols_up,
        rates,
        enter_back,
    )
    grad_keys = grad_keys_full.astype(bf16)
    grad_values = grad_values_full.astype(bf16)
    g_key = outer_sum(grad_keys, mix_key).astype(bf16)
    g_value = outer_sum(grad_values, mix_value).astype(bf16)
    g_recept = outer_sum(grad_recept, mix_recept).astype(bf16)
    sum_a = reduce_chunk(
        *unplace(
            [g_key, g_value, g_recept, g_output],
            places,
            ((0, hc), (hc, hc), (2 * hc, hc), (3 * hc, hc)),
            count,
        )
    )
    grad_key_one = dot(grad_keys, key_t)
    grad_value_one = dot(grad_values, value_t)
    grad_recept_one = dot(grad_recept, recept_t)
    grad_normed, mixer_small = blend_back(
        normed,
        before,
        (grad_key_one, grad_value_one, grad_recept_one),
        (blend_key, blend_value, blend_recept),
    )
    grad_first_gain = jnp.sum(grad_normed * scaled_one, axis=0)
    grad_first_bias = jnp.sum(grad_normed, axis=0)
    grad_tokens = grad_hidden + norm_back(grad_normed, scaled_one, inverse_one, first_gain)

    small = total_small(
        jnp.stack(
            [
                grad_first_gain,
                grad_first_bias,
                grad_second_gain,
                grad_second_bias,
                *mixer_small,
                *ffn_small,
                rate_small[0],
                rate_small[1],
            ]
        )
    )
    mine = lax.dynamic_slice_in_dim(small[9:], me * chan, chan, 1)

    def finish(part):
        size = lax.axis_size("dp")
        step = 2
        while step < size:
            part = part + lax.ppermute(part, "dp", [(i, i ^ step) for i in range(size)])
            step *= 2
        far = swap_core(part)
        first = jnp.where(core == 0, part, far)
        second = jnp.where(core == 0, far, part)

        def take(offset, length):
            return jnp.concatenate(
                [first[offset : offset + length], second[offset : offset + length]], 0
            ).astype(f32)

        return take

    take_a, take_b, take_c = finish(sum_a), finish(sum_b), finish(sum_c)
    return (
        block_out,
        grad_tokens,
        small[0],
        small[1],
        small[2],
        small[3],
        small[4],
        small[5],
        small[6],
        small[7],
        small[8],
        mine[0],
        mine[1],
        take_a(0, hc).T,
        take_a(hc, hc).T,
        take_a(2 * hc, hc).T,
        take_a(3 * hc, hc),
        take_b(0, hu).T,
        take_c(0, hu),
        take_b(hu, hc).T,
    )


def solution(mesh):
    rows = P(("dp", "mp"), None)
    cols = P(None, "mp")
    tall = P("mp", None)
    each = P("mp")
    return jax.shard_map(
        shards,
        mesh=mesh,
        in_specs=(rows, rows, P("dp", None))
        + (P(),) * 9
        + (each, each, cols, cols, cols, tall, cols, tall, cols),
        out_specs=(rows, rows) + (P(),) * 9 + (each, each, cols, cols, cols, tall, cols, tall, cols),
        check_vma=False,
    )
```

```python
import functools

import jax
import jax.numpy as jnp
from jax import lax
from jax.experimental import pallas as pl
from jax.experimental.pallas import tpu as pltpu
from jax.sharding import PartitionSpec as P

norm_eps = 1e-05
f32 = jnp.float32
bf16 = jnp.bfloat16


def bits_of(count):
    total = count.bit_length() - 1
    cube = (0, 2, 4) if total == 5 else (0, 1, 2)
    pre = tuple(b for b in range(total) if b not in cube)
    return pre, cube


def swap(value, bit):
    count = lax.axis_size("mp")
    return lax.ppermute(value, "mp", [(i, i ^ (1 << bit)) for i in range(count)])


def swap_core(value):
    count = lax.axis_size("dp")
    return lax.ppermute(value, "dp", [(i, i ^ 1) for i in range(count)])


def relative_ids(count):
    pre, (a, b, c) = bits_of(count)
    low = [0]
    for bit in pre:
        low = low + [i ^ (1 << bit) for i in low]
    x, y, z = 1 << a, 1 << b, 1 << c
    return [k ^ i for k in (0, x, y, z, x ^ y, y ^ z, x ^ z, x ^ y ^ z) for i in low]


def after(value, *earlier):
    return lax.optimization_barrier((value,) + earlier)[0]


class Gather:
    def __init__(self, part):
        self.v = part[None]

    def wide(self, *earlier):
        pre, _ = bits_of(lax.axis_size("mp"))
        v = after(self.v, *earlier) if earlier else self.v
        for bit in pre:
            far = swap(v, bit)
            v = jnp.concatenate([v, far], 0)
        self.v, self.seen = v, (far,)

    def near(self, *earlier):
        _, (a, b, c) = bits_of(lax.axis_size("mp"))
        v = after(self.v, *earlier) if earlier else self.v
        self.first = self.seen = (swap(v, a), swap(v, b), swap(v, c))

    def edge(self, *earlier):
        _, (a, b, c) = bits_of(lax.axis_size("mp"))
        x, y, z = self.first
        self.second = self.seen = (swap(y, a), swap(z, b), swap(x, c))

    def corner(self, *earlier):
        _, (a, b, c) = bits_of(lax.axis_size("mp"))
        _, yz, xz = self.second
        half = yz.shape[0] // 2
        self.third = self.seen = (swap(yz[:half], a), swap(xz[half:], b))
        self.own = jnp.concatenate((self.v,) + self.first + self.second + self.third, 0)

    def core(self):
        self.other = swap_core(self.own)


class Scatter:
    def __init__(self, own, other):
        self.own, self.far = own, swap_core(other)
        self.seen = (self.far,)

    def corner(self):
        count = lax.axis_size("mp")
        _, (a, b, c) = bits_of(count)
        part = self.own + self.far
        self.p = part.reshape((8, count // 8) + part.shape[1:])
        half = self.p.shape[1] // 2
        self.seen = (swap(self.p[7, :half], a), swap(self.p[7, half:], b))

    def edge(self):
        _, (a, b, c) = bits_of(lax.axis_size("mp"))
        p = self.p
        half = p.shape[1] // 2
        one, two = self.seen
        yz = jnp.concatenate([p[5, :half] + one, p[5, half:]], 0)
        xz = jnp.concatenate([p[6, :half], p[6, half:] + two], 0)
        self.seen = (swap(p[4], a), swap(yz, b), swap(xz, c))

    def near(self):
        _, (a, b, c) = bits_of(lax.axis_size("mp"))
        p = self.p
        y, z, x = p[2] + self.seen[0], p[3] + self.seen[1], p[1] + self.seen[2]
        self.seen = (swap(x, a), swap(y, b), swap(z, c))

    def wide(self):
        pre, _ = bits_of(lax.axis_size("mp"))
        v = self.p[0] + self.seen[0] + self.seen[1] + self.seen[2]
        for bit in reversed(pre):
            half = v.shape[0] // 2
            far = swap(v[half:], bit)
            v = v[:half] + far
        self.seen = (far,)
        self.sum = v[0]


def gather_small(value):
    count = lax.axis_size("mp")
    v = value[None]
    for bit in range(count.bit_length() - 1):
        v = jnp.concatenate([v, swap(v, bit)], 0)
    return v


def total_small(value):
    for axis in ("mp", "dp"):
        count = lax.axis_size(axis)
        for bit in range(count.bit_length() - 1):
            value = value + lax.ppermute(value, axis, [(i, i ^ (1 << bit)) for i in range(count)])
    return value


ANY = pl.BlockSpec(memory_space=pl.ANY)
SMEM = pl.BlockSpec(memory_space=pltpu.SMEM)


def cost(microseconds):
    return pl.CostEstimate(
        flops=0, bytes_accessed=int(microseconds * 3_000_000), transcendentals=0
    )


def place_kernel(pieces, count, places_ref, own_ref, other_ref, *rest):
    outs, sem = rest[:-1], rest[-1]
    copies = []
    for (offset, rows), out in zip(pieces, outs):
        for side, source in enumerate((own_ref, other_ref)):
            for j in range(count):
                target = pl.multiple_of(places_ref[side, j] * rows, 16)
                copies.append(
                    pltpu.make_async_copy(
                        source.at[j, pl.ds(offset, rows), :],
                        out.at[pl.ds(target, rows), :],
                        sem.at[len(copies)],
                    )
                )
    for copy in copies:
        copy.start()
    for copy in copies:
        copy.wait()


def place(own, other, places, pieces):
    count, _, width = own.shape
    return pl.pallas_call(
        functools.partial(place_kernel, pieces, count),
        out_shape=tuple(
            jax.ShapeDtypeStruct((2 * count * rows, width), own.dtype) for _, rows in pieces
        ),
        in_specs=[SMEM, ANY, ANY],
        out_specs=tuple(pl.BlockSpec(memory_space=pltpu.VMEM) for _ in pieces),
        scratch_shapes=[pltpu.SemaphoreType.DMA((2 * count * len(pieces),))],
        compiler_params=pltpu.CompilerParams(vmem_limit_bytes=40 * 2**20),
        cost_estimate=cost(4.0 * len(pieces)),
    )(places, own, other)


def unplace_kernel(pieces, count, places_ref, *rest):
    sources, (own_ref, other_ref, sem) = rest[:-3], rest[-3:]
    copies = []
    for (offset, rows), source in zip(pieces, sources):
        for side, out in enumerate((own_ref, other_ref)):
            for j in range(count):
                start = pl.multiple_of(places_ref[side, j] * rows, 16)
                copies.append(
                    pltpu.make_async_copy(
                        source.at[pl.ds(start, rows), :],
                        out.at[j, pl.ds(offset, rows), :],
                        sem.at[len(copies)],
                    )
                )
    for copy in copies:
        copy.start()
    for copy in copies:
        copy.wait()


def unplace(matrices, places, pieces, count):
    width = matrices[0].shape[1]
    height = sum(rows for _, rows in pieces)
    shape = jax.ShapeDtypeStruct((count, height, width), matrices[0].dtype)
    return pl.pallas_call(
        functools.partial(unplace_kernel, pieces, count),
        out_shape=(shape, shape),
        in_specs=[SMEM] + [pl.BlockSpec(memory_space=pltpu.VMEM)] * len(matrices),
        out_specs=(ANY, ANY),
        scratch_shapes=[pltpu.SemaphoreType.DMA((2 * count * len(pieces),))],
        compiler_params=pltpu.CompilerParams(vmem_limit_bytes=40 * 2**20),
        cost_estimate=cost(4.0 * len(pieces)),
    )(places, *matrices)


def tile_down(value_a, value_b, cols, powers):
    for k in range(3):
        factor = powers[k] * cols[:, k : k + 1]
        value_a = value_a + factor * pltpu.roll(value_a, 1 << k, 0)
        value_b = value_b + factor * pltpu.roll(value_b, 1 << k, 0)
    return value_a, value_b


def tile_up(value_a, value_b, cols, powers):
    for k in range(3):
        factor = powers[k] * cols[:, k : k + 1]
        value_a = value_a + factor * pltpu.roll(value_a, 8 - (1 << k), 0)
        value_b = value_b + factor * pltpu.roll(value_b, 8 - (1 << k), 0)
    return value_a, value_b


def forward_end_kernel(k_ref, v_ref, cols_ref, decay_ref, out_ref):
    rows, width = k_ref.shape
    rate = jnp.exp(decay_ref[0:1, :])
    powers = [jnp.exp(-rate * (1 << k)) for k in range(3)]
    climb = lax.broadcasted_iota(jnp.int32, (8, width), 0).astype(f32) + 1.0
    full = jnp.exp(-rate * climb)

    def body(t, carry):
        at = pl.ds(pl.multiple_of(t * 8, 8), 8)
        cols = cols_ref[at, :]
        growth = jnp.exp(k_ref[at, :])
        ya, yb = tile_down(growth * v_ref[at, :], growth, cols, powers)
        reach = full * cols[:, 3:4]
        ya = ya + reach * carry[0]
        yb = yb + reach * carry[1]
        return ya[7:8, :], yb[7:8, :]

    zero = jnp.zeros((1, width), f32)
    ya, yb = lax.fori_loop(0, rows // 8, body, (zero, zero))
    out_ref[0:1, :] = ya
    out_ref[1:2, :] = yb


def forward_kernel(k_ref, v_ref, r_ref, cols_ref, decay_ref, enter_ref, gated_ref, mixed_ref, a_ref, b_ref):
    rows, width = k_ref.shape
    rate = jnp.exp(decay_ref[0:1, :])
    bonus = decay_ref[1:2, :]
    powers = [jnp.exp(-rate * (1 << k)) for k in range(3)]
    place_in = lax.broadcasted_iota(jnp.int32, (8, width), 0)
    full = jnp.exp(-rate * (place_in.astype(f32) + 1.0))

    def body(t, carry):
        at = pl.ds(pl.multiple_of(t * 8, 8), 8)
        cols = cols_ref[at, :]
        keys = k_ref[at, :]
        values = v_ref[at, :]
        growth = jnp.exp(keys)
        ya, yb = tile_down(growth * values, growth, cols, powers)
        reach = full * cols[:, 3:4]
        ya = ya + reach * carry[0]
        yb = yb + reach * carry[1]
        keep = cols[:, 4:5]
        sa = keep * jnp.where(place_in == 0, carry[0], pltpu.roll(ya, 1, 0))
        sb = keep * jnp.where(place_in == 0, carry[1], pltpu.roll(yb, 1, 0))
        now = jnp.exp(bonus + keys)
        mixed = (sa + now * values) / (sb + now)
        a_ref[at, :] = sa
        b_ref[at, :] = sb
        mixed_ref[at, :] = mixed
        gated_ref[at, :] = jax.nn.sigmoid(r_ref[at, :]) * mixed
        return ya[7:8, :], yb[7:8, :]

    lax.fori_loop(0, rows // 8, body, (enter_ref[0:1, :], enter_ref[1:2, :]))


def backward_end_kernel(g_ref, k_ref, mixed_ref, b_ref, cols_ref, decay_ref, out_ref):
    rows, width = k_ref.shape
    rate = jnp.exp(decay_ref[0:1, :])
    bonus = decay_ref[1:2, :]
    powers = [jnp.exp(-rate * (1 << k)) for k in range(3)]
    place_in = lax.broadcasted_iota(jnp.int32, (8, width), 0)
    full = jnp.exp(-rate * (8.0 - place_in.astype(f32)))
    tiles = rows // 8

    def body(step, carry):
        at = pl.ds(pl.multiple_of((tiles - 1 - step) * 8, 8), 8)
        cols = cols_ref[at, :]
        now = jnp.exp(bonus + k_ref[at, :])
        xa = g_ref[at, :] / (b_ref[at, :] + now)
        ya, yb = tile_up(xa, -xa * mixed_ref[at, :], cols, powers)
        reach = full * cols[:, 3:4]
        ya = ya + reach * carry[0]
        yb = yb + reach * carry[1]
        return ya[0:1, :], yb[0:1, :]

    zero = jnp.zeros((1, width), f32)
    ya, yb = lax.fori_loop(0, tiles, body, (zero, zero))
    out_ref[0:1, :] = ya
    out_ref[1:2, :] = yb


def backward_kernel(
    g_ref, k_ref, v_ref, mixed_ref, a_ref, b_ref, cols_ref, decay_ref, enter_ref, gk_ref, gv_ref, small_ref
):
    rows, width = k_ref.shape
    rate = jnp.exp(decay_ref[0:1, :])
    bonus = decay_ref[1:2, :]
    powers = [jnp.exp(-rate * (1 << k)) for k in range(3)]
    place_in = lax.broadcasted_iota(jnp.int32, (8, width), 0)
    full = jnp.exp(-rate * (8.0 - place_in.astype(f32)))
    tiles = rows // 8

    def body(step, carry):
        at = pl.ds(pl.multiple_of((tiles - 1 - step) * 8, 8), 8)
        cols = cols_ref[at, :]
        keys = k_ref[at, :]
        values = v_ref[at, :]
        mixed = mixed_ref[at, :]
        sa, sb = a_ref[at, :], b_ref[at, :]
        now = jnp.exp(bonus + keys)
        growth = jnp.exp(keys)
        xa = g_ref[at, :] / (sb + now)
        ya, yb = tile_up(xa, -xa * mixed, cols, powers)
        reach = full * cols[:, 3:4]
        ya = ya + reach * carry[0]
        yb = yb + reach * carry[1]
        keep = cols[:, 4:5]
        after_a = keep * jnp.where(place_in == 7, carry[0], pltpu.roll(ya, 7, 0))
        after_b = keep * jnp.where(place_in == 7, carry[1], pltpu.roll(yb, 7, 0))
        share = xa * now
        bend = share * (values - mixed)
        gv_ref[at, :] = share + after_a * growth
        gk_ref[at, :] = bend + growth * (after_a * values + after_b)
        return (
            ya[0:1, :],
            yb[0:1, :],
            carry[2] + bend,
            carry[3] + after_a * sa + after_b * sb,
        )

    zero = jnp.zeros((8, width), f32)
    done = lax.fori_loop(0, tiles, body, (enter_ref[0:1, :], enter_ref[1:2, :], zero, zero))
    small_ref[0:1, :] = jnp.sum(done[3], axis=0, keepdims=True) * (-rate * jnp.exp(-rate))
    small_ref[1:2, :] = jnp.sum(done[2], axis=0, keepdims=True)


def call_whole(kernel, outs, *args):
    return pl.pallas_call(
        kernel,
        out_shape=outs,
        in_specs=[pl.BlockSpec(memory_space=pltpu.VMEM)] * len(args),
        out_specs=jax.tree.map(lambda _: pl.BlockSpec(memory_space=pltpu.VMEM), outs),
        compiler_params=pltpu.CompilerParams(vmem_limit_bytes=40 * 2**20),
        cost_estimate=cost(4.0),
    )(*args)


def dot(left, right):
    return jnp.dot(left, right, preferred_element_type=f32)


def outer_sum(left, right):
    return lax.dot_general(left, right, (((0,), (0,)), ((), ())), preferred_element_type=f32)


def against(left, weight):
    return lax.dot_general(left, weight, (((1,), (1,)), ((), ())), preferred_element_type=f32)


def normalize(source):
    centre = jnp.mean(source, axis=-1, keepdims=True)
    spread = source - centre
    inverse = lax.rsqrt(jnp.mean(spread * spread, axis=-1, keepdims=True) + norm_eps)
    return spread * inverse, inverse


def blend_pair(present, before, factor):
    return (present.astype(f32) * factor + before * (1.0 - factor)).astype(bf16)


def norm_back(grad, scaled, inverse, gain):
    h = grad * gain
    return inverse * (
        h
        - jnp.mean(h, axis=-1, keepdims=True)
        - scaled * jnp.mean(h * scaled, axis=-1, keepdims=True)
    )


def shards(
    tokens,
    cotangent,
    seq_lengths,
    first_gain,
    first_bias,
    second_gain,
    second_bias,
    blend_key,
    blend_value,
    blend_recept,
    channel_key,
    channel_recept,
    time_decay,
    time_first,
    weight_key,
    weight_value,
    weight_recept,
    weight_output,
    hidden_key,
    hidden_value,
    hidden_recept,
):
    count = lax.axis_size("mp")
    me = lax.axis_index("mp")
    core = lax.rem(lax.axis_index("dp"), 2)
    rows, width = tokens.shape
    group_rows = rows * count
    chan = weight_key.shape[1]
    units = hidden_key.shape[1]
    hc, hu = chan // 2, units // 2
    ids = relative_ids(count)
    shift_down = [(i, i + 1) for i in range(count - 1)]
    shift_up = [(i + 1, i) for i in range(count - 1)]

    def half_rows(matrix, size):
        return lax.dynamic_slice_in_dim(matrix, core * size, size, 0)

    def half_cols(matrix, size):
        return lax.dynamic_slice_in_dim(matrix, core * size, size, 1).T

    chunk_a = jnp.concatenate(
        [
            half_cols(weight_key, hc),
            half_cols(weight_value, hc),
            half_cols(weight_recept, hc),
            half_rows(weight_output, hc),
        ],
        0,
    )
    chunk_b = jnp.concatenate([half_cols(hidden_key, hu), half_cols(hidden_recept, hc)], 0)
    chunk_c = half_rows(hidden_value, hu)
    ga, gb, gc = Gather(chunk_a), Gather(chunk_b), Gather(chunk_c)
    ga.wide()
    ga.near()
    gb.wide(*ga.seen[:0])
    ga.edge()
    gb.near(*ga.first)
    ga.corner()
    ga.core()
    gc.wide(*gb.seen[:0])
    gb.edge()
    gc.near(*gb.first)
    gb.corner()
    gb.core()
    gc.edge()
    gc.corner()
    gc.core()
    own_a, own_b, own_c = ga.own, gb.own, gc.own
    other_a, other_b, other_c = ga.other, gb.other, gc.other
    ids_array = jnp.array(ids, jnp.int32)
    owners = jnp.bitwise_xor(ids_array, me)
    places = jnp.stack([owners * 2 + core, owners * 2 + 1 - core]).astype(jnp.int32)

    lengths = seq_lengths[0]
    ends = jnp.cumsum(lengths)

    def start_of(place):
        return jnp.sum(jnp.where(ends <= place[..., None], lengths, 0), axis=-1)

    def keep_of(place):
        return ((place > start_of(place)) & (place < group_rows)).astype(f32)

    here = me * rows + jnp.arange(rows, dtype=jnp.int32)
    keep_flat = keep_of(here)
    keep = keep_flat[:, None]
    keep_next = keep_of(here + 1)
    tiles = rows // 8

    def tile_cols(flags, up):
        f = flags.reshape(tiles, 8)
        if up:
            f = f[:, ::-1]
        one = f * (jnp.arange(8) >= 1)
        two = f * jnp.roll(f, 1, 1) * (jnp.arange(8) >= 2)
        four = f * jnp.roll(f, 1, 1) * jnp.roll(f, 2, 1) * jnp.roll(f, 3, 1) * (jnp.arange(8) >= 4)
        through = jnp.cumprod(f, axis=1)
        cols = jnp.stack([one, two, four, through, f, f, f, f], axis=-1)
        if up:
            cols = cols[:, ::-1]
        return cols.reshape(rows, 8)

    cols_down = tile_cols(keep_flat, False)
    cols_up = tile_cols(keep_next, True)

    small_rates = gather_small(jnp.stack([time_decay, time_first]))
    order = jnp.bitwise_xor(jnp.arange(count, dtype=jnp.int32), me)
    rates = jnp.moveaxis(jnp.take(small_rates, order, axis=0), 0, 1).reshape(2, width)
    rate = jnp.exp(rates[0])

    source = tokens.astype(f32)
    edge_row = lax.ppermute(tokens[-1:], "mp", shift_down).astype(f32)
    scaled_one, inverse_one = normalize(source)
    normed = (scaled_one * first_gain + first_bias).astype(bf16)
    edge = (normalize(edge_row)[0] * first_gain + first_bias).astype(bf16)
    before = jnp.concatenate([edge, normed[:-1]], 0).astype(f32) * keep
    mix_key = blend_pair(normed, before, blend_key)
    mix_value = blend_pair(normed, before, blend_value)
    mix_recept = blend_pair(normed, before, blend_recept)

    key_t, value_t, recept_t, output_w = place(
        own_a, other_a, places, ((0, hc), (hc, hc), (2 * hc, hc), (3 * hc, hc))
    )
    keys = against(mix_key, key_t)
    values = against(mix_value, value_t)
    recept = against(mix_recept, recept_t)

    pair = jax.ShapeDtypeStruct((2, width), f32)
    field = jax.ShapeDtypeStruct((rows, width), f32)
    sources = jnp.bitwise_xor(jnp.arange(count, dtype=jnp.int32), me)

    def fold(ends_all, valid, distance):
        weight = jnp.where(
            valid[:, None], jnp.exp(-rate[None] * (rows * distance[:, None]).astype(f32)), 0.0
        )
        return jnp.sum(ends_all * weight[:, None], axis=0)

    out_end = call_whole(forward_end_kernel, pair, keys, values, cols_down, rates)
    enter = fold(
        gather_small(out_end),
        (sources < me) & (start_of(me * rows - 1) < rows * (sources + 1)),
        jnp.maximum(me - 1 - sources, 0),
    )
    gated_full, mixed, state_a, state_b = call_whole(
        forward_kernel, (field, field, field, field), keys, values, recept, cols_down, rates, enter
    )
    gated = gated_full.astype(bf16)
    opened = jax.nn.sigmoid(recept)

    hidden = source + dot(gated, output_w)
    scaled_two, inverse_two = normalize(hidden)
    low = (scaled_two * second_gain + second_bias).astype(bf16)
    edge_two = lax.ppermute(low[-1:], "mp", shift_down)
    prior = jnp.concatenate([edge_two, low[:-1]], 0).astype(f32) * keep
    ffn_key_in = blend_pair(low, prior, channel_key)
    ffn_recept_in = blend_pair(low, prior, channel_recept)
    (hidden_recept_t,) = place(own_b, other_b, places, ((hu, hc),))
    hidden_key_t = jnp.concatenate([own_b[:, :hu], other_b[:, :hu]], 0).reshape(-1, width)
    hidden_value_w = jnp.concatenate([own_c, other_c], 0).reshape(-1, width)
    ffn_relu = jax.nn.relu(against(ffn_key_in, hidden_key_t))
    squared = jnp.square(ffn_relu).astype(bf16)
    gate = jax.nn.sigmoid(against(ffn_recept_in, hidden_recept_t))
    grad_out = cotangent.astype(f32)
    grad_carried = (grad_out * gate).astype(bf16)

    def split(matrix, size):
        parts = matrix.astype(bf16).reshape(2, count, size, width)
        return parts[0], parts[1]

    g_value_own, g_value_other = split(outer_sum(squared, grad_carried), hu)
    rc = Scatter(g_value_own, g_value_other)

    carried = dot(squared, hidden_value_w)
    block_out = (hidden + gate * carried).astype(bf16)
    grad_gate_pre = (grad_out * carried * gate * (1.0 - gate)).astype(bf16)
    grad_pre = (against(grad_carried, hidden_value_w) * 2.0 * ffn_relu).astype(bf16)
    rc.corner()
    grad_pre = after(grad_pre, rc.far)
    g_key_own, g_key_other = split(outer_sum(grad_pre, ffn_key_in), hu)
    g_recept_own, g_recept_other = unplace(
        [outer_sum(grad_gate_pre, ffn_recept_in).astype(bf16)], places, ((0, hc),), count
    )
    rb = Scatter(
        jnp.concatenate([g_key_own, g_recept_own], 1), jnp.concatenate([g_key_other, g_recept_other], 1)
    )
    grad_gate_pre = after(grad_gate_pre, *rc.seen)
    rc.edge()
    grad_key_two = dot(grad_pre, hidden_key_t)
    grad_recept_two = dot(grad_gate_pre, hidden_recept_t)

    def blend_back(present, earlier, grads, factors):
        direct = sum(g * f for g, f in zip(grads, factors))
        spill = sum(g * (1.0 - f) for g, f in zip(grads, factors)) * keep
        tail = lax.ppermute(spill[:1], "mp", shift_up)
        change = present.astype(f32) - earlier
        totals = [jnp.sum(g * change, axis=0) for g in grads]
        return direct + jnp.concatenate([spill[1:], tail], 0), totals

    grad_second, ffn_small = blend_back(
        low, prior, (grad_key_two, grad_recept_two), (channel_key, channel_recept)
    )
    grad_second = after(grad_second, *rc.seen, rb.far)
    rb.corner()
    rc.near()
    grad_second_gain = jnp.sum(grad_second * scaled_two, axis=0)
    grad_second_bias = jnp.sum(grad_second, axis=0)
    grad_hidden = grad_out + norm_back(grad_second, scaled_two, inverse_two, second_gain)
    grad_attended = grad_hidden.astype(bf16)

    g_output = outer_sum(gated, grad_attended).astype(bf16)
    grad_gated = against(grad_attended, output_w)
    grad_mixed = grad_gated * opened
    grad_recept = (grad_gated * mixed * opened * (1.0 - opened)).astype(bf16)
    grad_mixed = after(grad_mixed, *rb.seen, *rc.seen)
    rc.wide()
    rb.edge()
    back_end = call_whole(
        backward_end_kernel, pair, grad_mixed, keys, mixed, state_b, cols_up, rates
    )
    enter_back = fold(
        gather_small(back_end),
        (sources > me) & (start_of(sources * rows) <= rows * (me + 1)),
        jnp.maximum(sources - 1 - me, 0),
    )
    grad_keys_full, grad_values_full, rate_small = call_whole(
        backward_kernel,
        (field, field, pair),
        grad_mixed,
        keys,
        values,
        mixed,
        state_a,
        state_b,
        cols_up,
        rates,
        enter_back,
    )
    grad_keys = grad_keys_full.astype(bf16)
    grad_values = grad_values_full.astype(bf16)
    grad_keys = after(grad_keys, *rb.seen, *rc.seen)
    rb.near()
    g_key = outer_sum(grad_keys, mix_key).astype(bf16)
    g_value = outer_sum(grad_values, mix_value).astype(bf16)
    g_recept = outer_sum(grad_recept, mix_recept).astype(bf16)
    ra = Scatter(
        *unplace(
            [g_key, g_value, g_recept, g_output],
            places,
            ((0, hc), (hc, hc), (2 * hc, hc), (3 * hc, hc)),
            count,
        )
    )
    grad_keys = after(grad_keys, *rb.seen)
    rb.wide()
    grad_key_one = dot(grad_keys, key_t)
    grad_value_one = dot(grad_values, value_t)
    grad_recept_one = dot(grad_recept, recept_t)
    grad_normed, mixer_small = blend_back(
        normed,
        before,
        (grad_key_one, grad_value_one, grad_recept_one),
        (blend_key, blend_value, blend_recept),
    )
    ra.corner()
    ra.edge()
    ra.near()
    ra.wide()
    grad_first_gain = jnp.sum(grad_normed * scaled_one, axis=0)
    grad_first_bias = jnp.sum(grad_normed, axis=0)
    grad_tokens = grad_hidden + norm_back(grad_normed, scaled_one, inverse_one, first_gain)

    small = total_small(
        jnp.stack(
            [
                grad_first_gain,
                grad_first_bias,
                grad_second_gain,
                grad_second_bias,
                *mixer_small,
                *ffn_small,
                rate_small[0],
                rate_small[1],
            ]
        )
    )
    mine = lax.dynamic_slice_in_dim(small[9:], me * chan, chan, 1)

    def finish(part):
        size = lax.axis_size("dp")
        step = 2
        while step < size:
            part = part + lax.ppermute(part, "dp", [(i, i ^ step) for i in range(size)])
            step *= 2
        far = swap_core(part)
        first = jnp.where(core == 0, part, far)
        second = jnp.where(core == 0, far, part)

        def take(offset, length):
            return jnp.concatenate(
                [first[offset : offset + length], second[offset : offset + length]], 0
            ).astype(f32)

        return take

    take_a, take_b, take_c = finish(ra.sum), finish(rb.sum), finish(rc.sum)
    return (
        block_out,
        grad_tokens,
        small[0],
        small[1],
        small[2],
        small[3],
        small[4],
        small[5],
        small[6],
        small[7],
        small[8],
        mine[0],
        mine[1],
        take_a(0, hc).T,
        take_a(hc, hc).T,
        take_a(2 * hc, hc).T,
        take_a(3 * hc, hc),
        take_b(0, hu).T,
        take_c(0, hu),
        take_b(hu, hc).T,
    )


def solution(mesh):
    rows = P(("dp", "mp"), None)
    cols = P(None, "mp")
    tall = P("mp", None)
    each = P("mp")
    return jax.shard_map(
        shards,
        mesh=mesh,
        in_specs=(rows, rows, P("dp", None))
        + (P(),) * 9
        + (each, each, cols, cols, cols, tall, cols, tall, cols),
        out_specs=(rows, rows) + (P(),) * 9 + (each, each, cols, cols, cols, tall, cols, tall, cols),
        check_vma=False,
    )
```

```python
import functools

import jax
import jax.numpy as jnp
from jax import lax
from jax.experimental import pallas as pl
from jax.experimental.pallas import tpu as pltpu
from jax.sharding import PartitionSpec as P

norm_eps = 1e-05
f32 = jnp.float32
bf16 = jnp.bfloat16


def mp_size():
    return lax.axis_size("mp")


def swap(value, bit):
    return lax.ppermute(value, "mp", [(i, i ^ (1 << bit)) for i in range(mp_size())])


def swap_core(value):
    return lax.ppermute(value, "dp", [(i, i ^ 1) for i in range(lax.axis_size("dp"))])


def send(value, pairs):
    count = mp_size()
    flat = [(a * count + b, c * count + d) for (a, b), (c, d) in pairs]
    return lax.ppermute(value, ("dp", "mp"), flat)


def top_bit():
    return mp_size().bit_length() - 2


def cross_top(value, owners_send):
    count, bit = mp_size(), top_bit()
    pairs = []
    for d in range(lax.axis_size("dp")):
        for i in range(count):
            owner = (i >> bit) == (d & 1)
            if owner == owners_send:
                pairs.append(((d, i), (d, i ^ (1 << bit))))
    return send(value, pairs)


def neighbour_rows(value, step, cross):
    count = mp_size()
    pairs = []
    for d in range(lax.axis_size("dp")):
        for i in range(count):
            if 0 <= i + step < count:
                pairs.append(((d, i), (d ^ cross, i + step)))
    return send(value, pairs)


KEYS = (0, 1, 2, 4, 3, 6, 5, 7)


def low_ids():
    low = [0]
    for bit in range(3, top_bit()):
        low = low + [i ^ (1 << bit) for i in low]
    return low


def after(value, *earlier):
    return lax.optimization_barrier((value,) + earlier)[0]


class Gather:
    def __init__(self, part):
        self.part = part

    def wide(self, owner, *earlier):
        part = after(self.part, *earlier) if earlier else self.part
        far = cross_top(part, True)
        v = jnp.where(owner, part, far)[None]
        for bit in range(3, top_bit()):
            v = jnp.concatenate([v, swap(v, bit)], 0)
        self.v, self.seen = v, (far,)

    def near(self, *earlier):
        v = after(self.v, *earlier) if earlier else self.v
        self.first = self.seen = (swap(v, 0), swap(v, 1), swap(v, 2))

    def edge(self, *earlier):
        x, y, z = self.first
        if earlier:
            y = after(y, *earlier)
        self.second = self.seen = (swap(y, 0), swap(z, 1), swap(x, 2))

    def corner(self):
        _, yz, xz = self.second
        half = yz.shape[1] // 2
        self.third = self.seen = (swap(yz[:, :half], 0), swap(xz[:, half:], 1))
        self.pieces = (self.v,) + self.first + self.second + self.third


class Scatter:
    def __init__(self, pieces):
        self.p = pieces

    def corner(self):
        self.seen = (swap(self.p[7], 0), swap(self.p[8], 1))

    def edge(self):
        p = self.p
        half = p[7].shape[1]
        rest = p[5].shape[1] - half
        zero = jnp.zeros((), p[5].dtype)
        yz = p[5] + lax.pad(self.seen[0], zero, ((0, 0, 0), (0, rest, 0), (0, 0, 0)))
        xz = p[6] + lax.pad(self.seen[1], zero, ((0, 0, 0), (half, 0, 0), (0, 0, 0)))
        self.seen = (swap(p[4], 0), swap(yz, 1), swap(xz, 2))

    def near(self):
        p = self.p
        y, z, x = p[2] + self.seen[0], p[3] + self.seen[1], p[1] + self.seen[2]
        self.seen = (swap(x, 0), swap(y, 1), swap(z, 2))

    def wide(self):
        v = self.p[0] + self.seen[0] + self.seen[1] + self.seen[2]
        for bit in reversed(range(3, top_bit())):
            half = v.shape[0] // 2
            v = v[:half] + swap(v[half:], bit)
        v = v[0]
        far = cross_top(v, False)
        self.seen = (far,)
        self.sum = v + far

    def finish(self, owner):
        part = self.sum
        size = lax.axis_size("dp")
        step = 2
        while step < size:
            part = part + lax.ppermute(part, "dp", [(i, i ^ step) for i in range(size)])
            step *= 2
        self.result = jnp.where(owner, part, swap_core(part))


def gather_small(value):
    v = value[None]
    for bit in range(top_bit() + 1):
        v = jnp.concatenate([v, swap(v, bit)], 0)
    return v


def total_small(value):
    for axis in ("mp", "dp"):
        count = lax.axis_size(axis)
        for bit in range(count.bit_length() - 1):
            value = value + lax.ppermute(value, axis, [(i, i ^ (1 << bit)) for i in range(count)])
    return value


ANY = pl.BlockSpec(memory_space=pl.ANY)
SMEM = pl.BlockSpec(memory_space=pltpu.SMEM)
VMEM = pl.BlockSpec(memory_space=pltpu.VMEM)
STEP = 64


def call(kernel, outs, in_specs, args, scratch=(), out_specs=None, flops=0, micros=3.0, limit=44):
    return pl.pallas_call(
        kernel,
        out_shape=outs,
        in_specs=list(in_specs),
        out_specs=jax.tree.map(lambda _: VMEM, outs) if out_specs is None else out_specs,
        scratch_shapes=list(scratch),
        compiler_params=pltpu.CompilerParams(vmem_limit_bytes=limit * 2**20),
        cost_estimate=pl.CostEstimate(
            flops=0, bytes_accessed=int(micros * 3_000_000), transcendentals=0
        ),
    )(*args)


def shape(dims, dtype):
    return jax.ShapeDtypeStruct(tuple(dims), dtype)


def spans(many, height, offset, rows):
    half = height // 2
    found = []
    for k in range(8):
        for m in range(many):
            if k < 7:
                found.append((k, m, offset, rows, k * many + m, 0))
                continue
            if offset < half:
                size = min(offset + rows, half) - offset
                found.append((7, m, offset, size, k * many + m, 0))
            if offset + rows > half:
                begin = max(offset, half)
                found.append((8, m, begin - half, offset + rows - begin, k * many + m, begin - offset))
    return found


def count_spans(many, height, tensors):
    return sum(len(spans(many, height, *t)) for t in tensors)


def fetch(pieces, places, tensors, targets, sem, base=0):
    many = pieces[0].shape[0]
    height = pieces[0].shape[1]
    lists, number = [], base
    for (offset, rows), target in zip(tensors, targets):
        copies = []
        for piece, m, first, size, shard, inside in spans(many, height, offset, rows):
            row = pl.multiple_of(places[shard] * rows + inside, 16)
            copies.append(
                pltpu.make_async_copy(
                    pieces[piece].at[m, pl.ds(first, size), :], target.at[pl.ds(row, size), :], sem.at[number]
                )
            )
            number += 1
        for copy in copies:
            copy.start()
        lists.append(copies)
    return lists


def spread(pieces, places, tensor, source, sem, base, height):
    many = pieces[0].shape[0]
    offset, rows = tensor
    copies = []
    for piece, m, first, size, shard, inside in spans(many, height, offset, rows):
        row = pl.multiple_of(places[shard] * rows + inside, 16)
        copies.append(
            pltpu.make_async_copy(
                source.at[pl.ds(row, size), :],
                pieces[piece].at[m, pl.ds(first, size), :],
                sem.at[base + len(copies)],
            )
        )
    for copy in copies:
        copy.start()
    return copies


def wait(copies):
    for copy in copies:
        copy.wait()


def dot(left, right):
    return jnp.dot(left, right, preferred_element_type=f32)


def outer(left, right):
    return lax.dot_general(left, right, (((0,), (0,)), ((), ())), preferred_element_type=f32)


def against(left, weight):
    return lax.dot_general(left, weight, (((1,), (1,)), ((), ())), preferred_element_type=f32)


def loop(rows, body, start):
    return lax.fori_loop(0, rows // STEP, lambda i, c: body(pl.multiple_of(i * STEP, STEP), c), start)


def fold_rows(value):
    return jnp.sum(value.reshape(-1, 8, value.shape[-1]), axis=0)


def rate_factors(rates_ref, up):
    width = rates_ref.shape[1]
    rate = jnp.exp(rates_ref[0:1, :])
    powers = [jnp.exp(-rate * (1 << k)) for k in range(3)]
    place_in = lax.broadcasted_iota(jnp.int32, (8, width), 0)
    ahead = (8.0 - place_in.astype(f32)) if up else (place_in.astype(f32) + 1.0)
    return rate, powers, place_in, jnp.exp(-rate * ahead)


def climb(value_a, value_b, cols, powers, up):
    for k in range(3):
        factor = powers[k] * cols[:, k : k + 1]
        turn = 8 - (1 << k) if up else 1 << k
        value_a = value_a + factor * pltpu.roll(value_a, turn, 0)
        value_b = value_b + factor * pltpu.roll(value_b, turn, 0)
    return value_a, value_b


def mix_kernel(tensors, places, own_ref, far_ref, params_ref, cols_ref, rates_ref, *rest):
    pieces, rest = rest[:9], rest[9:]
    mk_ref, mv_ref, mr_ref, k_ref, v_ref, r_ref, end_ref, wk, wv, wr, sem = rest
    lists = fetch(pieces, places, tensors, (wk, wv, wr), sem)
    rows = own_ref.shape[1]
    for group, ref in enumerate((own_ref, far_ref)):

        def body(at, carry, group=group, ref=ref):
            present = ref[0, pl.ds(at, STEP), :].astype(f32)
            before = ref[1, pl.ds(at, STEP), :].astype(f32)
            for i, out in enumerate((mk_ref, mv_ref, mr_ref)):
                factor = params_ref[i : i + 1, :]
                out[pl.ds(group * rows + at, STEP), :] = (present * factor + before * (1.0 - factor)).astype(bf16)
            return carry

        loop(rows, body, 0)
    for copies, source, weight, out in zip(
        lists, (mk_ref, mv_ref, mr_ref), (wk, wv, wr), (k_ref, v_ref, r_ref)
    ):
        wait(copies)
        for n in range(0, weight.shape[0], 256):
            size = min(256, weight.shape[0] - n)
            out[:, n : n + size] = against(source[...], weight[n : n + size, :])
    _, powers, _, full = rate_factors(rates_ref, False)
    width = k_ref.shape[1]

    def one(t, group, carry):
        at = pl.ds(pl.multiple_of(group * rows + t * 8, 8), 8)
        cols = cols_ref[at, :]
        growth = jnp.exp(k_ref[at, :])
        ya, yb = climb(growth * v_ref[at, :], growth, cols, powers, False)
        reach = full * cols[:, 3:4]
        ya = ya + reach * carry[0]
        yb = yb + reach * carry[1]
        return ya[7:8, :], yb[7:8, :]

    def scan(t, carry):
        return one(t, 0, carry[0]), one(t, 1, carry[1])

    zero = jnp.zeros((1, width), f32)
    done = lax.fori_loop(0, rows // 8, scan, ((zero, zero), (zero, zero)))
    for group in range(2):
        for i in range(2):
            end_ref[2 * group + i : 2 * group + i + 1, :] = done[group][i]


def attend_kernel(tensors, places, k_ref, v_ref, r_ref, cols_ref, rates_ref, ends_ref, fade_ref, *rest):
    pieces, rest = rest[:9], rest[9:]
    gated_ref, mixed_ref, a_ref, b_ref, near_ref, far_ref, held, wo, sem = rest
    (copies,) = fetch(pieces, places, tensors, (wo,), sem)
    rows = k_ref.shape[0] // 2
    enter = jnp.sum(ends_ref[...] * fade_ref[...], axis=0)
    _, powers, place_in, full = rate_factors(rates_ref, False)
    bonus = rates_ref[1:2, :]

    def one(t, group, carry):
        at = pl.ds(pl.multiple_of(group * rows + t * 8, 8), 8)
        cols = cols_ref[at, :]
        keys = k_ref[at, :]
        values = v_ref[at, :]
        growth = jnp.exp(keys)
        ya, yb = climb(growth * values, growth, cols, powers, False)
        reach = full * cols[:, 3:4]
        ya = ya + reach * carry[0]
        yb = yb + reach * carry[1]
        keep = cols[:, 4:5]
        sa = keep * jnp.where(place_in == 0, carry[0], pltpu.roll(ya, 1, 0))
        sb = keep * jnp.where(place_in == 0, carry[1], pltpu.roll(yb, 1, 0))
        now = jnp.exp(bonus + keys)
        mixed = (sa + now * values) / (sb + now)
        a_ref[at, :] = sa
        b_ref[at, :] = sb
        mixed_ref[at, :] = mixed
        held[at, :] = jax.nn.sigmoid(r_ref[at, :]) * mixed
        return ya[7:8, :], yb[7:8, :]

    def scan(t, carry):
        return one(t, 0, carry[0]), one(t, 1, carry[1])

    lax.fori_loop(
        0, rows // 8, scan, ((enter[0:1], enter[1:2]), (enter[2:3], enter[3:4]))
    )

    def lower(at, carry):
        gated_ref[pl.ds(at, STEP), :] = held[pl.ds(at, STEP), :].astype(bf16)
        return carry

    loop(2 * rows, lower, 0)
    wait(copies)
    for n in range(0, wo.shape[1], 256):
        got = dot(gated_ref[...], wo[:, n : n + 256])
        near_ref[:, n : n + 256] = got[:rows]
        far_ref[:, n : n + 256] = got[rows:].astype(far_ref.dtype)


def norm_of(value):
    centre = jnp.mean(value, axis=-1, keepdims=True)
    moved = value - centre
    inverse = lax.rsqrt(jnp.mean(moved * moved, axis=-1, keepdims=True) + norm_eps)
    return moved * inverse, inverse


def second_norm_kernel(tokens_ref, near_ref, got_ref, params_ref, hidden_ref, low_ref):
    def body(at, carry):
        here = pl.ds(at, STEP)
        hidden = tokens_ref[here, :].astype(f32) + near_ref[here, :] + got_ref[here, :].astype(f32)
        hidden_ref[here, :] = hidden
        scaled, _ = norm_of(hidden)
        low_ref[here, :] = (scaled * params_ref[7:8, :] + params_ref[8:9, :]).astype(bf16)
        return carry

    loop(tokens_ref.shape[0], body, 0)


def earlier_rows(present, carry, keep):
    place_in = lax.broadcasted_iota(jnp.int32, present.shape, 0)
    return jnp.where(place_in == 0, carry, pltpu.roll(present, 1, 0)) * keep


def hidden_kernel(tensors, places, low_ref, low_far_ref, edge_ref, edge_far_ref, cols_ref, out_half_ref, params_ref, *rest):
    pieces, rest = rest[:9], rest[9:]
    fk_ref, fr_ref, relu_ref, squared_ref, gate_ref, carried_ref, wk, wr, sem = rest
    list_k, list_r = fetch(pieces, places, tensors, (wk, wr), sem)
    rows = low_ref.shape[0]
    for group, (ref, edge) in enumerate(((low_ref, edge_ref), (low_far_ref, edge_far_ref))):

        def body(at, carry, group=group, ref=ref):
            here = pl.ds(group * rows + at, STEP)
            present = ref[pl.ds(at, STEP), :].astype(f32)
            before = earlier_rows(present, carry, cols_ref[here, :][:, 4:5])
            for i, out in ((3, fk_ref), (4, fr_ref)):
                factor = params_ref[i : i + 1, :]
                out[here, :] = (present * factor + before * (1.0 - factor)).astype(bf16)
            return present[STEP - 1 :, :]

        loop(rows, body, edge[...].astype(f32))
    wait(list_r)
    for n in range(0, wr.shape[0], 256):
        gate = jax.nn.sigmoid(against(fr_ref[...], wr[n : n + 256, :]))
        gate_ref[:, n : n + 256] = gate
        carried_ref[:, n : n + 256] = (out_half_ref[:, n : n + 256].astype(f32) * gate).astype(bf16)
    wait(list_k)
    for n in range(0, wk.shape[0], 256):
        relu = jnp.maximum(against(fk_ref[...], wk[n : n + 256, :]), 0.0)
        relu_ref[:, n : n + 256] = relu.astype(bf16)
        squared_ref[:, n : n + 256] = (relu * relu).astype(bf16)


def value_grad_kernel(height, places, core_ref, squared_ref, mine_ref, far_ref, *rest):
    whole_ref, pieces, (held, sem) = rest[0], rest[1:10], rest[10:]
    half = mine_ref.shape[1]
    rows = mine_ref.shape[0] // 2
    for flag in range(2):

        @pl.when(core_ref[0] == flag)
        def _():
            whole_ref[:, flag * half : (flag + 1) * half] = mine_ref[...]
            whole_ref[:rows, (1 - flag) * half : (2 - flag) * half] = far_ref[rows:, :]
            whole_ref[rows:, (1 - flag) * half : (2 - flag) * half] = far_ref[:rows, :]

    units = squared_ref.shape[1]
    for n in range(0, units, 256):
        held[n : n + 256, :] = outer(squared_ref[:, n : n + 256], whole_ref[...]).astype(bf16)
    wait(spread(pieces, places, (0, height), held, sem, 0, height))


def value_kernel(tensors, places, core_ref, squared_ref, whole_ref, relu_ref, *rest):
    pieces, rest = rest[:9], rest[9:]
    keep_ref, send_ref, pre_ref, wv, sem = rest
    (copies,) = fetch(pieces, places, tensors, (wv,), sem)
    wait(copies)
    half = keep_ref.shape[1]
    for side in range(2):
        for n in range(0, half, 256):
            got = dot(squared_ref[...], wv[:, side * half + n : side * half + n + 256])

            @pl.when(core_ref[0] == side)
            def _():
                keep_ref[:, n : n + 256] = got

            @pl.when(core_ref[0] != side)
            def _():
                send_ref[:, n : n + 256] = got.astype(bf16)

    for n in range(0, wv.shape[0], 256):
        got = against(whole_ref[...], wv[n : n + 256, :])
        pre_ref[:, n : n + 256] = (got * 2.0 * relu_ref[:, n : n + 256].astype(f32)).astype(bf16)


def key_grad_kernel(tensors, height, places, pre_ref, fk_ref, *rest):
    sources, rest = rest[:9], rest[9:]
    back_ref, pieces, (wk, held, sem, sem_out) = rest[0], rest[1:10], rest[10:]
    (copies,) = fetch(sources, places, tensors, (wk,), sem)
    for n in range(0, wk.shape[0], 256):
        held[n : n + 256, :] = outer(pre_ref[:, n : n + 256], fk_ref[...]).astype(bf16)
    out = spread(pieces, places, (0, height), held, sem_out, 0, height)
    wait(copies)
    for n in range(0, back_ref.shape[1], 256):
        back_ref[:, n : n + 256] = dot(pre_ref[...], wk[:, n : n + 256])
    wait(out)


def shift_back(spill_ref, direct_ref, near_ref, far_ref, first_ref, rows):
    for group in range(2):
        first_ref[group : group + 1, :] = spill_ref[group * rows : group * rows + 1, :]

        def body(i, carry, group=group):
            at = pl.multiple_of(rows - (i + 1) * STEP, STEP)
            here = pl.ds(group * rows + at, STEP)
            spill = spill_ref[here, :]
            place_in = lax.broadcasted_iota(jnp.int32, spill.shape, 0)
            passed = jnp.where(place_in == STEP - 1, carry, pltpu.roll(spill, STEP - 1, 0))
            total = direct_ref[here, :] + passed
            if group == 0:
                near_ref[pl.ds(at, STEP), :] = total
            else:
                far_ref[pl.ds(at, STEP), :] = total.astype(bf16)
            return spill[0:1, :]

        lax.fori_loop(0, rows // STEP, body, jnp.zeros((1, spill_ref.shape[1]), f32))


def gate_back_kernel(
    tensors, places, keep_ref, got_ref, out_half_ref, gate_ref, back_ref, low_ref, low_far_ref, edge_ref, edge_far_ref,
    cols_ref, params_ref, *rest
):
    pieces, rest = rest[:9], rest[9:]
    pre_ref, added_ref, near_ref, far_ref, first_ref, totals_ref, wr, back_r, direct, spill, sem = rest
    (copies,) = fetch(pieces, places, tensors, (wr,), sem)
    rows = low_ref.shape[0]
    width = low_ref.shape[1]

    for group in range(2):

        def gates(at, carry, group=group):
            here = pl.ds(group * rows + at, STEP)
            there = pl.ds((1 - group) * rows + at, STEP)
            carried = keep_ref[here, :] + got_ref[there, :].astype(f32)
            gate = gate_ref[here, :]
            added = gate * carried
            added_ref[here, :] = added
            pre_ref[here, :] = (out_half_ref[here, :].astype(f32) * added * (1.0 - gate)).astype(bf16)
            return carry

        loop(rows, gates, 0)
    wait(copies)
    for n in range(0, width, 256):
        back_r[:, n : n + 256] = dot(pre_ref[...], wr[:, n : n + 256])
    zero = jnp.zeros((8, width), f32)
    sums = (zero, zero)
    for group, (ref, edge) in enumerate(((low_ref, edge_ref), (low_far_ref, edge_far_ref))):

        def body(at, carry, group=group, ref=ref):
            here = pl.ds(group * rows + at, STEP)
            present = ref[pl.ds(at, STEP), :].astype(f32)
            keep = cols_ref[here, :][:, 4:5]
            change = present - earlier_rows(present, carry[0], keep)
            one, two = back_ref[here, :], back_r[here, :]
            key, recept = params_ref[3:4, :], params_ref[4:5, :]
            direct[here, :] = one * key + two * recept
            spill[here, :] = (one * (1.0 - key) + two * (1.0 - recept)) * keep
            return (
                present[STEP - 1 :, :],
                carry[1] + fold_rows(one * change),
                carry[2] + fold_rows(two * change),
            )

        done = loop(rows, body, (edge[...].astype(f32),) + sums)
        sums = done[1:]
    for i in range(2):
        totals_ref[i : i + 1, :] = jnp.sum(sums[i], axis=0, keepdims=True)
    shift_back(spill, direct, near_ref, far_ref, first_ref, rows)


def norm_back_rows(grad, source, gain):
    scaled, inverse = norm_of(source)
    h = grad * gain
    back = inverse * (
        h
        - jnp.mean(h, axis=-1, keepdims=True)
        - scaled * jnp.mean(h * scaled, axis=-1, keepdims=True)
    )
    return back, scaled


def norm_back_kernel(row, low, source_ref, near_ref, got_ref, tail_ref, tail_far_ref, base_ref, params_ref, *outs):
    out_ref, totals_ref = outs[0], outs[-1]
    rows, width = source_ref.shape

    def body(at, carry):
        here = pl.ds(at, STEP)
        grad = near_ref[here, :] + got_ref[here, :].astype(f32)
        last = lax.broadcasted_iota(jnp.int32, grad.shape, 0) + at == rows - 1
        grad = grad + jnp.where(last, tail_ref[...] + tail_far_ref[...], 0.0)
        back, scaled = norm_back_rows(grad, source_ref[here, :].astype(f32), params_ref[row : row + 1, :])
        total = base_ref[here, :].astype(f32) + back
        out_ref[here, :] = total
        if low:
            outs[1][here, :] = total.astype(bf16)
        return carry[0] + fold_rows(grad * scaled), carry[1] + fold_rows(grad)

    zero = jnp.zeros((8, width), f32)
    done = loop(rows, body, (zero, zero))
    for i in range(2):
        totals_ref[i : i + 1, :] = jnp.sum(done[i], axis=0, keepdims=True)


def gated_back_kernel(
    tensors, places, ga_ref, ga_far_ref, k_ref, r_ref, mixed_ref, b_ref, cols_ref, rates_ref, *rest
):
    pieces, rest = rest[:9], rest[9:]
    grad_ref, recept_ref, end_ref, wo, sem = rest
    (copies,) = fetch(pieces, places, tensors, (wo,), sem)
    rows = ga_ref.shape[0]
    width = k_ref.shape[1]
    wait(copies)
    for group, ref in enumerate((ga_ref, ga_far_ref)):
        for n in range(0, width, 256):
            grad_ref[group * rows : (group + 1) * rows, n : n + 256] = against(ref[...], wo[n : n + 256, :])

    def body(at, carry):
        here = pl.ds(at, STEP)
        grad = grad_ref[here, :]
        opened = jax.nn.sigmoid(r_ref[here, :])
        grad_mixed = grad * opened
        recept_ref[here, :] = (grad_mixed * mixed_ref[here, :] * (1.0 - opened)).astype(bf16)
        grad_ref[here, :] = grad_mixed
        return carry

    loop(2 * rows, body, 0)
    _, powers, _, full = rate_factors(rates_ref, True)
    bonus = rates_ref[1:2, :]
    tiles = rows // 8

    def one(t, group, carry):
        at = pl.ds(pl.multiple_of(group * rows + (tiles - 1 - t) * 8, 8), 8)
        cols = cols_ref[at, :]
        now = jnp.exp(bonus + k_ref[at, :])
        xa = grad_ref[at, :] / (b_ref[at, :] + now)
        ya, yb = climb(xa, -xa * mixed_ref[at, :], cols, powers, True)
        reach = full * cols[:, 3:4]
        ya = ya + reach * carry[0]
        yb = yb + reach * carry[1]
        return ya[0:1, :], yb[0:1, :]

    def scan(t, carry):
        return one(t, 0, carry[0]), one(t, 1, carry[1])

    zero = jnp.zeros((1, width), f32)
    done = lax.fori_loop(0, tiles, scan, ((zero, zero), (zero, zero)))
    for group in range(2):
        for i in range(2):
            end_ref[2 * group + i : 2 * group + i + 1, :] = done[group][i]


def recur_back_kernel(
    grad_ref, k_ref, v_ref, mixed_ref, a_ref, b_ref, cols_ref, rates_ref, ends_ref, fade_ref,
    gk_ref, gv_ref, small_ref, held_k, held_v
):
    rows = k_ref.shape[0] // 2
    width = k_ref.shape[1]
    enter = jnp.sum(ends_ref[...] * fade_ref[...], axis=0)
    rate, powers, place_in, full = rate_factors(rates_ref, True)
    bonus = rates_ref[1:2, :]
    tiles = rows // 8

    def one(t, group, carry):
        at = pl.ds(pl.multiple_of(group * rows + (tiles - 1 - t) * 8, 8), 8)
        cols = cols_ref[at, :]
        keys = k_ref[at, :]
        values = v_ref[at, :]
        mixed = mixed_ref[at, :]
        now = jnp.exp(bonus + keys)
        growth = jnp.exp(keys)
        sb = b_ref[at, :]
        xa = grad_ref[at, :] / (sb + now)
        ya, yb = climb(xa, -xa * mixed, cols, powers, True)
        reach = full * cols[:, 3:4]
        ya = ya + reach * carry[0]
        yb = yb + reach * carry[1]
        keep = cols[:, 4:5]
        after_a = keep * jnp.where(place_in == 7, carry[0], pltpu.roll(ya, 7, 0))
        after_b = keep * jnp.where(place_in == 7, carry[1], pltpu.roll(yb, 7, 0))
        share = xa * now
        bend = share * (values - mixed)
        held_v[at, :] = share + after_a * growth
        held_k[at, :] = bend + growth * (after_a * values + after_b)
        return (
            ya[0:1, :],
            yb[0:1, :],
            carry[2] + bend,
            carry[3] + after_a * a_ref[at, :] + after_b * sb,
        )

    def scan(t, carry):
        return one(t, 0, carry[0]), one(t, 1, carry[1])

    zero = jnp.zeros((8, width), f32)
    done = lax.fori_loop(
        0,
        tiles,
        scan,
        ((enter[0:1], enter[1:2], zero, zero), (enter[2:3], enter[3:4], zero, zero)),
    )
    small_ref[0:1, :] = jnp.sum(done[0][3] + done[1][3], axis=0, keepdims=True) * (-rate * jnp.exp(-rate))
    small_ref[1:2, :] = jnp.sum(done[0][2] + done[1][2], axis=0, keepdims=True)

    def lower(at, carry):
        here = pl.ds(at, STEP)
        gk_ref[here, :] = held_k[here, :].astype(bf16)
        gv_ref[here, :] = held_v[here, :].astype(bf16)
        return carry

    loop(2 * rows, lower, 0)


def mix_grad_kernel(
    tensors, height, places, mk_ref, mv_ref, mr_ref, gk_ref, gv_ref, gr_ref, gated_ref, ga_ref, ga_far_ref, pre_ref,
    fr_ref, *rest
):
    pieces, (held, sem) = rest[:9], rest[9:]
    rows = ga_ref.shape[0]
    many = pieces[0].shape[0]
    base, copies = 0, []
    pairs = ((gk_ref, mk_ref), (gv_ref, mv_ref), (gr_ref, mr_ref), (gated_ref, None), (pre_ref, fr_ref))
    for i, (tensor, (left, right)) in enumerate(zip(tensors, pairs)):
        for n in range(0, held.shape[1], 256):
            if right is not None:
                got = outer(left[:, n : n + 256], right[...])
            else:
                got = outer(left[:rows, n : n + 256], ga_ref[...]) + outer(left[rows:, n : n + 256], ga_far_ref[...])
            held[i, n : n + 256, :] = got.astype(bf16)
        copies += spread(pieces, places, tensor, held.at[i], sem, base, height)
        base = len(copies)
    wait(copies)


def mix_back_kernel(tensors, places, gk_ref, gv_ref, gr_ref, own_ref, other_ref, cols_ref, params_ref, *rest):
    pieces, rest = rest[:9], rest[9:]
    near_ref, far_ref, first_ref, totals_ref, wk, wv, wr, back, direct, spill, sem = rest
    lists = fetch(pieces, places, tensors, (wk, wv, wr), sem)
    rows, width = own_ref.shape[1:]
    for i, (copies, source, weight) in enumerate(zip(lists, (gk_ref, gv_ref, gr_ref), (wk, wv, wr))):
        wait(copies)
        for n in range(0, width, 256):
            back[i, :, n : n + 256] = dot(source[...], weight[:, n : n + 256])
    zero = jnp.zeros((8, width), f32)
    sums = (zero, zero, zero)
    for group, ref in enumerate((own_ref, other_ref)):

        def body(at, carry, group=group, ref=ref):
            here = pl.ds(group * rows + at, STEP)
            keep = cols_ref[here, :][:, 4:5]
            change = ref[0, pl.ds(at, STEP), :].astype(f32) - ref[1, pl.ds(at, STEP), :].astype(f32)
            through = jnp.zeros((STEP, width), f32)
            aside = jnp.zeros((STEP, width), f32)
            found = []
            for i in range(3):
                grad = back[i, here, :]
                factor = params_ref[i : i + 1, :]
                through = through + grad * factor
                aside = aside + grad * (1.0 - factor)
                found.append(carry[i] + fold_rows(grad * change))
            direct[here, :] = through
            spill[here, :] = aside * keep
            return tuple(found)

        sums = loop(rows, body, sums)
    for i in range(3):
        totals_ref[i : i + 1, :] = jnp.sum(sums[i], axis=0, keepdims=True)
    shift_back(spill, direct, near_ref, far_ref, first_ref, rows)


def shards(
    tokens,
    cotangent,
    seq_lengths,
    first_gain,
    first_bias,
    second_gain,
    second_bias,
    blend_key,
    blend_value,
    blend_recept,
    channel_key,
    channel_recept,
    time_decay,
    time_first,
    weight_key,
    weight_value,
    weight_recept,
    weight_output,
    hidden_key,
    hidden_value,
    hidden_recept,
):
    count = mp_size()
    me = lax.axis_index("mp")
    core = lax.rem(lax.axis_index("dp"), 2)
    owner = lax.shift_right_logical(me, top_bit()) == core
    rows, width = tokens.shape
    group_rows = rows * count
    chan = weight_key.shape[1]
    units = hidden_key.shape[1]
    share = count // 2
    half, deep = share * chan, share * units
    many = share // 8
    both = 2 * rows

    height_a, height_b, height_c = 4 * chan, units + chan, units
    ga = Gather(jnp.concatenate([weight_key.T, weight_value.T, weight_recept.T, weight_output], 0))
    gb = Gather(jnp.concatenate([hidden_key.T, hidden_recept.T], 0))
    gc = Gather(hidden_value)
    ga.wide(owner)
    ga.near()
    gb.wide(owner)
    ga.edge()
    gb.near(*ga.first)
    ga.corner()
    gc.wide(owner)
    gb.edge()
    gc.near(*gb.first)
    gb.corner()
    gc.edge()
    gc.corner()
    at_k, at_v, at_r, at_o = [(i * chan, chan) for i in range(4)]
    at_hk, at_hr, at_hv = (0, units), (units, chan), (0, units)
    low = low_ids()
    ids = jnp.array([k ^ i for k in KEYS for i in low], jnp.int32)
    places = jnp.bitwise_xor(ids, jnp.bitwise_and(me, share - 1)).astype(jnp.int32)
    core_word = core.astype(jnp.int32)[None]

    own_lengths = seq_lengths[0]
    far_lengths = swap_core(own_lengths.astype(f32)).astype(jnp.int32)
    groups = (own_lengths, far_lengths)

    def start_of(lengths, place):
        ends = jnp.cumsum(lengths)
        return jnp.sum(jnp.where(ends <= place[..., None], lengths, 0), axis=-1)

    def keep_of(lengths, place):
        return ((place > start_of(lengths, place)) & (place < group_rows)).astype(f32)

    here = me * rows + jnp.arange(rows, dtype=jnp.int32)
    tiles = rows // 8

    def tile_cols(flags, up):
        f = flags.reshape(tiles, 8)
        if up:
            f = f[:, ::-1]
        one = f * (jnp.arange(8) >= 1)
        two = f * jnp.roll(f, 1, 1) * (jnp.arange(8) >= 2)
        four = f * jnp.roll(f, 1, 1) * jnp.roll(f, 2, 1) * jnp.roll(f, 3, 1) * (jnp.arange(8) >= 4)
        through = jnp.cumprod(f, axis=1)
        cols = jnp.stack([one, two, four, through, f, f, f, f], axis=-1)
        if up:
            cols = cols[:, ::-1]
        return cols.reshape(rows, 8)

    cols_down = jnp.concatenate([tile_cols(keep_of(n, here), False) for n in groups], 0)
    cols_up = jnp.concatenate([tile_cols(keep_of(n, here + 1), True) for n in groups], 0)
    keep = keep_of(own_lengths, here)[:, None]

    small_rates = gather_small(jnp.stack([time_decay, time_first]))
    mine = jnp.bitwise_xor(jnp.arange(share, dtype=jnp.int32) + core * share, me)
    rates = jnp.moveaxis(jnp.take(small_rates, mine, axis=0), 0, 1).reshape(2, half)
    rate = jnp.exp(rates[0])
    sources = jnp.bitwise_xor(jnp.arange(count, dtype=jnp.int32), me)

    def fade_of(valid, distance):
        faded = jnp.exp(-rate[None] * (rows * jnp.maximum(distance, 0)[:, None]).astype(f32))
        parts = [jnp.where(v[:, None], faded, 0.0) for v in valid]
        return jnp.stack([parts[0], parts[0], parts[1], parts[1]], axis=1)

    fade_down = fade_of(
        [(sources < me) & (start_of(n, me * rows - 1) < rows * (sources + 1)) for n in groups],
        me - 1 - sources,
    )
    fade_up = fade_of(
        [(sources > me) & (start_of(n, sources * rows) <= rows * (me + 1)) for n in groups],
        sources - 1 - me,
    )

    params = jnp.stack(
        [
            blend_key,
            blend_value,
            blend_recept,
            channel_key,
            channel_recept,
            first_gain,
            first_bias,
            second_gain,
            second_bias,
        ]
        + [jnp.zeros_like(first_gain)] * 7
    )
    edge_row = neighbour_rows(tokens[-1:], 1, 0).astype(f32)
    normed = (norm_of(tokens.astype(f32))[0] * first_gain + first_bias).astype(bf16)
    edge = (norm_of(edge_row)[0] * first_gain + first_bias).astype(bf16)
    before = (jnp.concatenate([edge, normed[:-1]], 0).astype(f32) * keep).astype(bf16)
    near_pair = jnp.stack([normed, before])
    far_pair = swap_core(near_pair)
    far_cotangent = swap_core(cotangent)
    out_half = jnp.concatenate(
        [lax.dynamic_slice_in_dim(c, core * half, half, 1) for c in (cotangent, far_cotangent)], 0
    )

    weight = lambda n: pltpu.VMEM((n, width), bf16)
    sems = lambda height, *t: pltpu.SemaphoreType.DMA((count_spans(many, height, t),))
    field = shape((both, half), f32)
    low_field = shape((both, half), bf16)
    wide_low = shape((both, width), bf16)
    ends = shape((4, half), f32)

    mk, mv, mr, keys, values, recept, end_down = call(
        functools.partial(mix_kernel, (at_k, at_v, at_r)),
        (wide_low, wide_low, wide_low, field, field, field, ends),
        [SMEM] + [VMEM] * 5 + [ANY] * 9,
        (places, near_pair, far_pair, params, cols_down, rates) + ga.pieces,
        [weight(half)] * 3 + [sems(height_a, at_k, at_v, at_r)],
        micros=9.0,
    )
    gated, mixed, state_a, state_b, near_att, far_att = call(
        functools.partial(attend_kernel, (at_o,)),
        (low_field, field, field, field, shape((rows, width), f32), shape((rows, width), bf16)),
        [SMEM] + [VMEM] * 7 + [ANY] * 9,
        (places, keys, values, recept, cols_down, rates, gather_small(end_down), fade_down) + ga.pieces,
        [pltpu.VMEM((both, half), f32), weight(half), sems(height_a, at_o)],
        micros=8.0,
    )
    hidden, lows = call(
        second_norm_kernel,
        (shape((rows, width), f32), shape((rows, width), bf16)),
        [VMEM] * 4,
        (tokens, near_att, swap_core(far_att), params),
        micros=2.0,
    )
    low_edge, low_edge_far = neighbour_rows(lows[-1:], 1, 0), neighbour_rows(lows[-1:], 1, 1)
    lows_far = swap_core(lows)

    fk, fr, relu, squared, gate, mine_carried = call(
        functools.partial(hidden_kernel, (at_hk, at_hr)),
        (wide_low, wide_low, shape((both, deep), bf16), shape((both, deep), bf16), field, low_field),
        [SMEM] + [VMEM] * 7 + [ANY] * 9,
        (places, lows, lows_far, low_edge, low_edge_far, cols_down, out_half, params) + gb.pieces,
        [weight(deep), weight(half), sems(height_b, at_hk, at_hr)],
        micros=9.0,
    )

    def piece_shapes(height):
        whole, part = shape((many, height, width), bf16), shape((many, height // 2, width), bf16)
        return (whole,) * 7 + (part, shape((many, height - height // 2, width), bf16))

    got = call(
        functools.partial(value_grad_kernel, units),
        (wide_low,) + piece_shapes(units),
        [SMEM, SMEM] + [VMEM] * 3,
        (places, core_word, squared, mine_carried, swap_core(mine_carried)),
        [weight(deep), sems(units, at_hv)],
        out_specs=(VMEM,) + (ANY,) * 9,
        micros=6.0,
    )
    grad_carried = got[0]
    rc = Scatter(got[1:])
    rc.corner()
    keep_carried, send_carried, grad_pre = call(
        functools.partial(value_kernel, (at_hv,)),
        (field, low_field, shape((both, deep), bf16)),
        [SMEM, SMEM] + [VMEM] * 3 + [ANY] * 9,
        (places, core_word, squared, grad_carried, relu) + gc.pieces,
        [weight(deep), sems(height_c, at_hv)],
        micros=9.0,
    )
    got_carried = swap_core(send_carried)
    grad_pre = after(grad_pre, *rc.seen)
    rc.edge()
    got = call(
        functools.partial(key_grad_kernel, (at_hk,), units),
        (shape((both, width), f32),) + piece_shapes(units),
        [SMEM] + [VMEM] * 2 + [ANY] * 9,
        (places, grad_pre, fk) + gb.pieces,
        [weight(deep), weight(deep), sems(height_b, at_hk), sems(units, at_hk)],
        out_specs=(VMEM,) + (ANY,) * 9,
        micros=9.0,
    )
    back_key = got[0]
    rb = Scatter(got[1:])
    rb.corner()
    back_key = after(back_key, *rc.seen)
    rc.near()
    gate_pre, added, near_two, far_two, first_two, totals_two = call(
        functools.partial(gate_back_kernel, (at_hr,)),
        (
            low_field,
            field,
            shape((rows, width), f32),
            shape((rows, width), bf16),
            shape((2, width), f32),
            shape((2, width), f32),
        ),
        [SMEM] + [VMEM] * 11 + [ANY] * 9,
        (
            places,
            keep_carried,
            got_carried,
            out_half,
            gate,
            back_key,
            lows,
            lows_far,
            low_edge,
            low_edge_far,
            cols_down,
            params,
        )
        + gb.pieces,
        [weight(half)] + [pltpu.VMEM((both, width), f32)] * 3 + [sems(height_b, at_hr)],
        micros=6.0,
    )
    tails = (neighbour_rows(first_two[:1], -1, 0), neighbour_rows(first_two[1:], -1, 1))
    got_two = swap_core(far_two)
    near_two = after(near_two, *rb.seen)
    rb.edge()
    grad_hidden, grad_att, totals_norm = call(
        functools.partial(norm_back_kernel, 7, True),
        (shape((rows, width), f32), shape((rows, width), bf16), shape((2, width), f32)),
        [VMEM] * 7,
        (hidden, near_two, got_two) + tails + (cotangent, params),
        micros=3.0,
    )
    grad_att_far = swap_core(grad_att)
    added_far = swap_core(added[rows:])
    sides = jnp.where(core == 0, jnp.stack([added[:rows], added_far]), jnp.stack([added_far, added[:rows]]))
    block_out = (hidden + jnp.concatenate([sides[0], sides[1]], 1)).astype(bf16)

    grad_att_far = after(grad_att_far, *rc.seen)
    rc.wide()
    grad_mixed, grad_recept, end_up = call(
        functools.partial(gated_back_kernel, (at_o,)),
        (field, low_field, ends),
        [SMEM] + [VMEM] * 8 + [ANY] * 9,
        (places, grad_att, grad_att_far, keys, recept, mixed, state_b, cols_up, rates) + ga.pieces,
        [weight(half), sems(height_a, at_o)],
        micros=6.0,
    )
    all_up = after(gather_small(end_up), *rb.seen)
    rb.near()
    grad_keys, grad_values, rate_small = call(
        recur_back_kernel,
        (low_field, low_field, shape((2, half), f32)),
        [VMEM] * 10,
        (grad_mixed, keys, values, mixed, state_a, state_b, cols_up, rates, all_up, fade_up),
        [pltpu.VMEM((both, half), f32)] * 2,
        micros=6.0,
    )
    grad_keys = after(grad_keys, *rb.seen, *rc.seen)
    rb.wide()
    height = 5 * chan
    tensors = tuple((i * chan, chan) for i in range(5))
    ra = Scatter(
        call(
            functools.partial(mix_grad_kernel, tensors, height),
            piece_shapes(height),
            [SMEM] + [VMEM] * 11,
            (
                places,
                mk,
                mv,
                mr,
                grad_keys,
                grad_values,
                grad_recept,
                gated,
                grad_att,
                grad_att_far,
                gate_pre,
                fr,
            ),
            [pltpu.VMEM((5, half, width), bf16), sems(height, *tensors)],
            out_specs=(ANY,) * 9,
            micros=7.0,
        )
    )
    ra.corner()
    near_one, far_one, first_one, totals_one = call(
        functools.partial(mix_back_kernel, (at_k, at_v, at_r)),
        (
            shape((rows, width), f32),
            shape((rows, width), bf16),
            shape((2, width), f32),
            shape((3, width), f32),
        ),
        [SMEM] + [VMEM] * 7 + [ANY] * 9,
        (places, grad_keys, grad_values, grad_recept, near_pair, far_pair, cols_down, params) + ga.pieces,
        [weight(half)] * 3
        + [pltpu.VMEM((3, both, width), f32)]
        + [pltpu.VMEM((both, width), f32)] * 2
        + [sems(height_a, at_k, at_v, at_r)],
        micros=9.0,
    )
    tails = (neighbour_rows(first_one[:1], -1, 0), neighbour_rows(first_one[1:], -1, 1))
    got_one = swap_core(far_one)
    near_one = after(near_one, *rb.seen)
    rb.finish(owner)
    rc.finish(owner)
    ra.edge()
    grad_tokens, totals_first = call(
        functools.partial(norm_back_kernel, 5, False),
        (shape((rows, width), f32), shape((2, width), f32)),
        [VMEM] * 7,
        (tokens, near_one, got_one) + tails + (grad_hidden, params),
        micros=3.0,
    )

    rate_wide = jnp.zeros((2, 2, half), f32)
    rate_wide = lax.dynamic_update_slice(rate_wide, rate_small[:, None], (0, core, 0)).reshape(2, width)
    small = total_small(jnp.concatenate([totals_first, totals_norm, totals_one, totals_two, rate_wide], 0))
    rate_mine = lax.dynamic_slice_in_dim(small[9:], me * chan, chan, 1)
    ra.near()
    ra.wide()
    ra.finish(owner)

    def take(scatter, tensor):
        offset, size = tensor
        return scatter.result[offset : offset + size].astype(f32)

    return (
        block_out,
        grad_tokens,
        small[0],
        small[1],
        small[2],
        small[3],
        small[4],
        small[5],
        small[6],
        small[7],
        small[8],
        rate_mine[0],
        rate_mine[1],
        take(ra, tensors[0]).T,
        take(ra, tensors[1]).T,
        take(ra, tensors[2]).T,
        take(ra, tensors[3]),
        take(rb, at_hk).T,
        take(rc, at_hv),
        take(ra, tensors[4]).T,
    )


def solution(mesh):
    rows = P(("dp", "mp"), None)
    cols = P(None, "mp")
    tall = P("mp", None)
    each = P("mp")
    return jax.shard_map(
        shards,
        mesh=mesh,
        in_specs=(rows, rows, P("dp", None))
        + (P(),) * 9
        + (each, each, cols, cols, cols, tall, cols, tall, cols),
        out_specs=(rows, rows) + (P(),) * 9 + (each, each, cols, cols, cols, tall, cols, tall, cols),
        check_vma=False,
    )
```
